256 devices in a mesh: dp: 8 (over z_hi, y), mp: 32 (over x, z_lo, core).
Axes of the slice: x: 4, y: 4, z: 8 (z_hi: 2, z_lo: 4; z = z_hi * 4 + z_lo), core: 2. Of those that a mesh axis runs over, the one named last changes fastest.
Arguments:
- tokens: bfloat16 [8192, 2560], P('dp'), may hold values from -6 to 6
- cotangent: bfloat16 [8192, 10240], P('dp', 'mp'), may hold values from -0.0625 to 0.0625
- saved_panels: bfloat16 [2048, 8192], P(None, 'mp'), may hold values from -0.125 to 0.125
- owners: int32 [32, 2], replicated, may hold values from 0 to 7, as said below
- row_growth: bfloat16 [2560, 2048], P(None, 'dp'), may hold values from -0.125 to 0.125
- col_growth: bfloat16 [10240, 8192], P('mp', 'dp'), may hold values from -0.0625 to 0.0625
Outputs:
- grown_out: bfloat16 [8192, 10240], P('dp', 'mp')
- grad_grown: float32 [2560, 10240], P('dp', 'mp')
- grad_row_growth: float32 [2560, 2048], P('mp', 'dp')
- grad_col_growth: float32 [10240, 8192], P('mp', 'dp')
The draws below stay inside these ranges and needn't reach their ends.
Inputs may be any that keep to these rules, and one draw needn't show every extreme that they name: `owners`: column 0 is a rank below 8, column 1 a section below 4; every pair of rank and section names exactly one panel.
All inputs are finite; a program needn't handle non-finite values.
Results may differ from the reference program's by a relative error of at most 0.006.
Values may be sent and summed in bfloat16 or wider, within the bound.
No kernel may reach another device: no remote copies, remote signals or barrier semaphores. Data moves between devices by JAX's collectives and lax.ppermute only.
A program may use at most 128 MiB of HBM per device.

```python
import jax
import jax.numpy as jnp

D_NEW = 2560
D_OLD = 2048
F_NEW = 10240
F_OLD = 8192
SECTIONS = 4
TOKENS = 8192
N_MP = 32


def draw_owners(key, part):
    key = jax.random.fold_in(key, 7)
    shuffled = jax.random.permutation(key, N_MP).astype(jnp.int32)
    tp_count = N_MP // SECTIONS
    tp_rank = shuffled % tp_count
    pp_section = shuffled // tp_count
    return jnp.stack([tp_rank, pp_section], axis=1).astype(jnp.int32)


def shard_levels(key, dims, shards, low, top_value):
    gain, own = 1.0, jax.random.fold_in(key, 6)
    for axis_at, shards_of in shards:
        heights = jnp.exp(jax.random.uniform(jax.random.fold_in(own, axis_at), (shards_of,), jnp.float32, low / len(shards), top_value / len(shards)))
        gain = gain * jnp.repeat(heights, dims[axis_at] // shards_of).reshape([-1 if axis == axis_at else 1 for axis in range(len(dims))])
    return gain


def noise(stream_key, shape, spread, most, cuts=(), kind=jnp.bfloat16):
    gain = shard_levels(stream_key, shape, cuts, -0.22, 0.18) if cuts else 1.0
    result = jax.random.normal(stream_key, shape, jnp.float32) * spread * gain
    return jnp.minimum(jnp.maximum(result, -most), most).astype(kind)


def setup_inputs(seed: int = 0) -> dict:
    keys = jax.random.split(jax.random.key(seed), 7)
    return {
        "tokens": noise(keys[0], (TOKENS, D_NEW), 1.0, 6.0, ((0, 8),)),
        "cotangent": noise(keys[1], (TOKENS, F_NEW), TOKENS ** -0.5, 0.0625, ((0, 8), (1, 32))),
        "saved_panels": noise(keys[2], (D_OLD, F_OLD), D_OLD ** -0.5, 0.125, ((1, 32),)),
        "owners": draw_owners(jax.random.fold_in(keys[6], 71), 0),
        "row_growth": noise(keys[4], (D_NEW, D_OLD), D_OLD ** -0.5, 0.125, ((1, 8),)),
        "col_growth": noise(keys[5], (F_NEW, F_OLD), F_OLD ** -0.5, 0.0625, ((0, 32), (1, 8))),
    }


def reference(tokens, cotangent, saved_panels, owners, row_growth, col_growth):
    panel_width = F_OLD // N_MP
    tp_count = N_MP // SECTIONS
    slot_of = (owners[:, 1] * tp_count + owners[:, 0]).astype(jnp.int32)
    blocks = saved_panels.reshape(D_OLD, N_MP, panel_width)
    source_weight = jnp.take(blocks, slot_of, axis=1).reshape(D_OLD, F_OLD)
    inner = jnp.dot(source_weight, col_growth.T, preferred_element_type=jnp.float32).astype(jnp.bfloat16)
    grown = jnp.dot(row_growth, inner, preferred_element_type=jnp.float32).astype(jnp.bfloat16)
    grown_out = jnp.dot(tokens, grown, preferred_element_type=jnp.float32).astype(jnp.bfloat16)
    grad_grown = jnp.dot(tokens.T, cotangent, preferred_element_type=jnp.float32)
    grad_rounded = grad_grown.astype(jnp.bfloat16)
    back_inner = jnp.dot(row_growth.T, grad_rounded, preferred_element_type=jnp.float32).astype(jnp.bfloat16)
    grad_col = jnp.dot(back_inner.T, source_weight, preferred_element_type=jnp.float32)
    grad_row = jnp.dot(grad_rounded, inner.T, preferred_element_type=jnp.float32)
    return grown_out, grad_grown, grad_row, grad_col
```

```python
import jax
import jax.numpy as jnp
from jax import lax
from jax.sharding import PartitionSpec as P

SECTIONS = 4
ZH, NY = 2, 4
NX, NZ, NC = 4, 4, 2
Y_GROUPS = [[h * NY + y for y in range(NY)] for h in range(ZH)]
X_GROUPS = [[(x * NZ + z) * NC + c for x in range(NX)] for z in range(NZ) for c in range(NC)]
Z_GROUPS = [[(x * NZ + z) * NC + c for z in range(NZ)] for x in range(NX) for c in range(NC)]
SWAP_ZH = [(i, (i + NY) % (ZH * NY)) for i in range(ZH * NY)]
SWAP_CORE = [(m, m ^ 1) for m in range(NX * NZ * NC)]
BF, F32 = jnp.bfloat16, jnp.float32


def dot(a, b, dims, kind=F32):
    return lax.dot_general(a, b, (dims, ((), ())), preferred_element_type=F32).astype(kind)


def exchange(blocks, axis, groups=None):
    return lax.all_to_all(blocks, axis, 0, 0, axis_index_groups=groups)


def gather(block, axis, groups, count):
    return exchange(jnp.broadcast_to(block[None], (count,) + block.shape), axis, groups)


def pick(blocks, index):
    return lax.dynamic_index_in_dim(blocks, index, 0, keepdims=False)


def reduce_rows(term, z_hi):
    blocks = term.reshape(ZH, NY, -1, term.shape[1]).transpose(1, 0, 2, 3).astype(BF)
    part = exchange(blocks, "dp", Y_GROUPS).astype(F32).sum(axis=0)
    other = lax.ppermute(pick(part, 1 - z_hi).astype(BF), "dp", SWAP_ZH)
    return pick(part, z_hi) + other.astype(F32)


def gather_rows(block, z_hi):
    other = lax.ppermute(block, "dp", SWAP_ZH)
    pair = jnp.where(z_hi == 0, jnp.stack([block, other]), jnp.stack([other, block]))
    return gather(pair, "dp", Y_GROUPS, NY)


def source_part(saved, slot_of, z_hi, y):
    width = saved.shape[1]
    sub = saved.shape[0] // (NX * NZ * NC * NY)
    rows = saved.reshape(NC, NX, NZ, NY, sub, width)
    mine = lax.dynamic_index_in_dim(rows, y, 3, keepdims=False)
    mine = mine.transpose(1, 2, 0, 3, 4).reshape(NX * NZ * NC, sub, width)
    slots = exchange(mine, "mp")
    panels = jnp.take(slots, slot_of, axis=0).reshape(ZH, NY, -1, sub, width)
    parts = exchange(pick(panels, z_hi), "dp", Y_GROUPS)
    chunk = parts.transpose(0, 2, 1, 3).reshape(NY * sub, -1)
    plane = gather(chunk, "mp", Z_GROUPS, NZ)
    plane = gather(plane.reshape(-1, chunk.shape[1]), "mp", X_GROUPS, NX)
    half = plane.reshape(-1, chunk.shape[1])
    other = lax.ppermute(half, "mp", SWAP_CORE)
    core = lax.axis_index("mp") % NC
    return jnp.where(
        core == 0, jnp.concatenate([half, other]), jnp.concatenate([other, half])
    )


def shards(tokens, cotangent, saved_panels, owners, row_growth, col_growth):
    dp_index, mp_index = lax.axis_index("dp"), lax.axis_index("mp")
    mp_count = lax.axis_size("mp")
    z_hi, y = dp_index // NY, dp_index % NY
    slot_of = owners[:, 1] * (mp_count // SECTIONS) + owners[:, 0]
    old = row_growth.shape[1]
    hidden = cotangent.shape[1]

    strip = old // mp_count
    strips = pick(row_growth.T.reshape(mp_count, strip, -1), mp_index)
    strips = gather(strips, "dp", None, ZH * NY).reshape(ZH * NY * strip, -1)
    mixed = dot(strips, tokens, ((1,), (1,)), BF)
    mixed = lax.all_gather(mixed, "mp", axis=0, tiled=True)

    part_weight = source_part(saved_panels, slot_of, z_hi, y)

    grad = reduce_rows(dot(tokens, cotangent, ((0,), (0,))), z_hi)
    grad_all = gather_rows(grad.astype(BF), z_hi).reshape(-1, hidden)
    ordered_growth = (
        row_growth.reshape(ZH, NY, -1, old).transpose(1, 0, 2, 3).reshape(-1, old)
    )
    back = gather_rows(dot(ordered_growth, grad_all, ((0,), (0,)), BF), z_hi)
    back = back.transpose(1, 0, 2, 3).reshape(-1, hidden)
    grad_col = dot(back, part_weight, ((0,), (0,)))

    inner = reduce_rows(dot(part_weight, col_growth, ((1,), (1,))), z_hi).astype(BF)
    inner_all = gather_rows(inner, z_hi)

    grow = dot(grad_all, inner, ((1,), (1,)))
    rows = grow.shape[0] // mp_count
    grow = grow.reshape(NY, ZH, -1, rows, old).transpose(1, 0, 2, 3, 4)
    grow = grow.reshape(NX * NZ, NC, rows, old)
    core = mp_index % NC
    keep = lax.dynamic_index_in_dim(grow, core, 1, keepdims=False)
    give = lax.dynamic_index_in_dim(grow, 1 - core, 1, keepdims=False)
    keep = keep + lax.ppermute(give.astype(BF), "mp", SWAP_CORE).astype(F32)
    keep = keep.reshape(NX, NZ, rows, old).astype(BF)
    keep = exchange(keep, "mp", X_GROUPS).astype(F32).sum(axis=0)
    grad_row = exchange(keep, "mp", Z_GROUPS).sum(axis=0)

    inner_all = inner_all.transpose(1, 0, 2, 3).reshape(ZH * NY, mp_count, strip, hidden)
    inner_all = inner_all.transpose(1, 0, 2, 3).reshape(-1, hidden)
    grown_out = dot(mixed, inner_all, ((0,), (0,)), BF)
    return (grown_out, grad, grad_row, grad_col)


def solution(mesh):
    in_specs = (P("dp", None), P("dp", "mp"), P(None, "mp"), P(), P(None, "dp"), P("mp", "dp"))
    out_specs = (P("dp", "mp"), P("dp", "mp"), P("mp", "dp"), P("mp", "dp"))
    return jax.shard_map(shards, mesh=mesh, in_specs=in_specs, out_specs=out_specs, check_vma=False)
```

```python
import jax
import jax.numpy as jnp
from jax import lax
from jax.sharding import PartitionSpec as P

SECTIONS = 4
ZH, NY = 2, 4
NX, NZ, NC = 4, 4, 2
MP = NX * NZ * NC
PLANE_GROUPS = [[(x * NZ + z) * NC + c for x in range(NX) for z in range(NZ)] for c in range(NC)]
SWAP_ZH = [(i, (i + NY) % (ZH * NY)) for i in range(ZH * NY)]
SWAP_CORE = [(m, m ^ 1) for m in range(MP)]
BF, F32 = jnp.bfloat16, jnp.float32


def shift_y(k):
    return [(h * NY + y, h * NY + (y + k) % NY) for h in range(ZH) for y in range(NY)]


def shift_x(k):
    return [
        ((x * NZ + z) * NC + c, ((x + k) % NX * NZ + z) * NC + c)
        for x in range(NX) for z in range(NZ) for c in range(NC)
    ]


def flip_z(k):
    return [
        ((x * NZ + z) * NC + c, (x * NZ + (z ^ k)) * NC + c)
        for x in range(NX) for z in range(NZ) for c in range(NC)
    ]


def dot(a, b, dims, kind=F32):
    return lax.dot_general(a, b, (dims, ((), ())), preferred_element_type=F32).astype(kind)


def pick(blocks, index, axis=0):
    return lax.dynamic_index_in_dim(blocks, index, axis, keepdims=False)


def choose(index, cases):
    out = cases[-1]
    for at in range(len(cases) - 1):
        out = jnp.where(index == at, cases[at], out)
    return out


def exchange_y(block_for):
    got = {k: lax.ppermute(block_for(k), "dp", shift_y(k)) for k in (2, 1, 3)}
    return [None, got[1], got[2], got[3]]


def sum_dp(block_for):
    got = exchange_y(lambda k: block_for(k).astype(BF))
    part = block_for(0) + got[1].astype(F32) + got[2].astype(F32) + got[3].astype(F32)
    return part + lax.ppermute(part.astype(BF), "dp", SWAP_ZH).astype(F32)


def gather_y(pair):
    got = exchange_y(lambda k: pair)
    return [pair] + got[1:]


def natural(by_k, y):
    out = jnp.stack([choose((y - j) % NY, by_k) for j in range(NY)], axis=1)
    return out.reshape(-1, out.shape[-1])


def source_blocks(saved, slot_of, z_hi, y):
    width = saved.shape[1]
    sub = saved.shape[0] // (MP * NY)
    rows = saved.reshape(NC, NX, NZ, NY, sub, width)
    mine = pick(rows, y, 3).transpose(1, 2, 0, 3, 4).reshape(MP, sub, width)
    slots = lax.all_to_all(mine, "mp", 0, 0)
    panels = jnp.take(slots, slot_of, axis=0).reshape(ZH, NY, -1, sub, width)
    panels = pick(panels, z_hi)
    got = exchange_y(lambda k: pick(panels, (y + k) % NY))
    got[0] = pick(panels, y)
    chunk = jnp.stack([choose((y - j) % NY, got) for j in range(NY)])
    chunk = chunk.transpose(0, 2, 1, 3).reshape(NY * sub, -1)
    z = lax.axis_index("mp") // NC % NZ
    got = [chunk] + [lax.ppermute(chunk, "mp", flip_z(k)) for k in (1, 2, 3)]
    strip = jnp.concatenate([choose(z ^ j, got) for j in range(NZ)])
    got = {k: lax.ppermute(strip, "mp", shift_x(k)) for k in (2, 1, 3)}
    got[0] = strip
    return [jnp.stack([got[k], lax.ppermute(got[k], "mp", SWAP_CORE)]) for k in range(NX)]


def shards(tokens, cotangent, saved_panels, owners, row_growth, col_growth):
    dp_index, mp_index = lax.axis_index("dp"), lax.axis_index("mp")
    z_hi, y = dp_index // NY, dp_index % NY
    x, core = mp_index // (NZ * NC), mp_index % NC
    slot_of = owners[:, 1] * (MP // SECTIONS) + owners[:, 0]
    old = row_growth.shape[1]
    hidden = cotangent.shape[1]

    strip = old // MP
    strips = pick(row_growth.T.reshape(MP, strip, -1), mp_index)
    strips = lax.all_gather(strips, "dp", axis=0, tiled=True)
    mixed = dot(strips, tokens, ((1,), (1,)), BF)
    mixed = lax.all_gather(mixed, "mp", axis=0, tiled=True)

    source = source_blocks(saved_panels, slot_of, z_hi, y)

    term = dot(tokens, cotangent, ((0,), (0,))).reshape(ZH, NY, -1, hidden)
    grads = sum_dp(lambda k: pick(term, (y + k) % NY, 1))
    grad = pick(grads, z_hi)
    grad_all = natural(gather_y(grads.astype(BF)), y)
    back = dot(row_growth, grad_all, ((0,), (0,)), BF)
    other = lax.ppermute(back, "dp", SWAP_ZH)
    back = gather_y(jnp.where(z_hi == 0, jnp.stack([back, other]), jnp.stack([other, back])))
    rows_for = [choose((y - x + k) % NY, back) for k in range(NX)]
    rows_for = [jnp.where(core == 0, r, r[::-1]) for r in rows_for]
    grad_col = dot(
        jnp.stack(rows_for).reshape(-1, hidden),
        jnp.stack(source).reshape(-1, source[0].shape[-1]),
        ((0,), (0,)),
    )

    terms = jnp.stack([dot(s, col_growth, ((2,), (1,))) for s in source])

    def inner_for(k):
        both = pick(terms, (x - y - k) % NX)
        return jnp.where(core == 0, both, both[::-1])

    inners = sum_dp(inner_for).astype(BF)
    inner_all = natural(gather_y(inners), y)

    grow = dot(grad_all, pick(inners, z_hi), ((1,), (1,)))
    grow = grow.reshape(NX * NZ, NC, -1, old)
    give = lax.ppermute(pick(grow, 1 - core, 1).astype(BF), "mp", SWAP_CORE)
    keep = (pick(grow, core, 1) + give.astype(F32)).astype(BF)
    groups = [g for g in PLANE_GROUPS]
    grad_row = lax.all_to_all(keep, "mp", 0, 0, axis_index_groups=groups).astype(F32).sum(axis=0)

    inner_all = inner_all.reshape(ZH * NY, MP, strip, hidden)
    inner_all = inner_all.transpose(1, 0, 2, 3).reshape(-1, hidden)
    grown_out = dot(mixed, inner_all, ((0,), (0,)), BF)
    return (grown_out, grad, grad_row, grad_col)


def solution(mesh):
    in_specs = (P("dp", None), P("dp", "mp"), P(None, "mp"), P(), P(None, "dp"), P("mp", "dp"))
    out_specs = (P("dp", "mp"), P("dp", "mp"), P("mp", "dp"), P("mp", "dp"))
    return jax.shard_map(shards, mesh=mesh, in_specs=in_specs, out_specs=out_specs, check_vma=False)
```

```python
import jax
import jax.numpy as jnp
from jax import lax
from jax.experimental import pallas as pl
from jax.experimental.pallas import tpu as pltpu
from jax.sharding import PartitionSpec as P

SECTIONS = 4
ZH, NY = 2, 4
NX, NZ, NC = 4, 4, 2
MP = NX * NZ * NC
PLANE_GROUPS = [[(x * NZ + z) * NC + c for x in range(NX) for z in range(NZ)] for c in range(NC)]
SWAP_ZH = [(i, (i + NY) % (ZH * NY)) for i in range(ZH * NY)]
SWAP_CORE = [(m, m ^ 1) for m in range(MP)]
BF, F32 = jnp.bfloat16, jnp.float32
NN, NT, TN = ((1,), (0,)), ((1,), (1,)), ((0,), (0,))


def shift_y(k):
    return [(h * NY + y, h * NY + (y + k) % NY) for h in range(ZH) for y in range(NY)]


def shift_x(k):
    return [
        ((x * NZ + z) * NC + c, ((x + k) % NX * NZ + z) * NC + c)
        for x in range(NX) for z in range(NZ) for c in range(NC)
    ]


def flip_z(k):
    return [
        ((x * NZ + z) * NC + c, (x * NZ + (z ^ k)) * NC + c)
        for x in range(NX) for z in range(NZ) for c in range(NC)
    ]


def dot(a, b, dims):
    return lax.dot_general(a, b, (dims, ((), ())), preferred_element_type=F32)


def pick(blocks, index, axis=0):
    return lax.dynamic_index_in_dim(blocks, index, axis, keepdims=False)


def choose(index, cases):
    out = cases[-1]
    for at in range(len(cases) - 1):
        out = jnp.where(index == at, cases[at], out)
    return out


def call(body, place, arrays, outs, flops, scratch=(), grid=None, in_specs=None, out_specs=None):
    size = lambda s: s.size * s.dtype.itemsize
    whole = pl.BlockSpec(memory_space=pltpu.VMEM)
    return pl.pallas_call(
        body,
        out_shape=outs,
        grid=grid or (),
        in_specs=[pl.BlockSpec(memory_space=pltpu.SMEM)] + (in_specs or [whole] * len(arrays)),
        out_specs=out_specs or jax.tree.map(lambda _: whole, outs),
        scratch_shapes=list(scratch),
        compiler_params=pltpu.CompilerParams(vmem_limit_bytes=40 * 2**20),
        cost_estimate=pl.CostEstimate(
            flops=flops,
            bytes_accessed=sum(map(size, arrays)) + sum(map(size, jax.tree.leaves(outs))),
            transcendentals=0,
        ),
    )(place, *arrays)


def struct(shape, kind):
    return jax.ShapeDtypeStruct(shape, kind)


def put(value, k, at, outs):
    for case, out in enumerate(outs):
        @pl.when(k == case)
        def _():
            out[at] = value.astype(out.dtype)


def grad_body(place, tokens, cot, *outs):
    step = pl.program_id(0)
    both = dot(cot[...], tokens[...], NN)
    n = both.shape[1] // 2
    for half in range(2):
        block = 2 * step + half
        put(
            both[:, half * n:(half + 1) * n],
            lax.rem(lax.rem(block, NY) - place[0] + NY, NY),
            block // NY,
            outs,
        )


def grad_terms(place, tokens, cot):
    n = tokens.shape[1] // (ZH * NY)
    hidden = cot.shape[0]
    shape = (ZH, hidden, n)
    outs = [struct(shape, F32)] + [struct(shape, BF)] * (NY - 1)
    full = pl.BlockSpec(shape, lambda s: (0, 0, 0))
    return call(
        grad_body, place, (tokens, cot), outs, 2 * tokens.size * hidden,
        grid=(ZH * NY // 2,),
        in_specs=[
            pl.BlockSpec((tokens.shape[0], 2 * n), lambda s: (0, s)),
            pl.BlockSpec(cot.shape, lambda s: (0, 0)),
        ],
        out_specs=[full] * NY,
    )


def back_body(place, grown, *refs):
    grads, out = refs[:NY], refs[NY]
    n = grads[0].shape[2]
    total = jnp.zeros(out.shape, F32)
    for k in range(NY):
        for h in range(ZH):
            first = (h * NY + lax.rem(place[0] - k + NY, NY)) * n
            total += dot(grads[k][h], grown[pl.ds(pl.multiple_of(first, n), n), :], NN)
    out[...] = total.astype(out.dtype)


def back_block(place, row_growth, grads):
    hidden, old = grads[0].shape[1], row_growth.shape[1]
    return call(
        back_body, place, (row_growth, *grads), struct((hidden, old), BF),
        2 * row_growth.size * hidden,
    )


def inner_body(place, col, *refs):
    source, outs = refs[:2 * NX], refs[2 * NX:]
    for k in range(NX):
        for c in range(NC):
            block = dot(col[...], source[2 * k + c][...], NT)
            where = lax.rem(place[2] - k - place[0] + 2 * NX, NX)
            put(block, where, place[3] ^ c, outs)


def inner_terms(place, col, source):
    hidden, rows = col.shape[0], source[0].shape[0]
    shape = (ZH, hidden, rows)
    outs = [struct(shape, F32)] + [struct(shape, BF)] * (NY - 1)
    return call(inner_body, place, (col, *source), outs, 2 * col.size * rows * len(source))


def col_body(place, *refs):
    source, back, out, held = refs[:2 * NX], refs[2 * NX:2 * NX + NY], refs[-2], refs[-1]
    for k in range(NY):
        held[k] = back[k][...]
    total = jnp.zeros(out.shape, F32)
    for k in range(NX):
        for c in range(NC):
            at = lax.rem(place[0] - place[2] + k + NY, NY)
            total += dot(held[at, place[3] ^ c], source[2 * k + c][...], NN)
    out[...] = total


def col_grad(place, source, back):
    hidden, rows = back[0].shape[1:]
    return call(
        col_body, place, (*source, *back), struct((hidden, source[0].shape[1]), F32),
        2 * hidden * sum(s.size for s in source),
        scratch=[pltpu.VMEM((NY, *back[0].shape), BF)],
    )


def row_body(place, inner, *refs):
    grads, keep, give = refs[:NY], refs[NY], refs[NY + 1]
    rows = keep.shape[1]
    for k in range(NY):
        for h in range(ZH):
            block = dot(grads[k][h], inner[...], TN)
            at = (h * NY + lax.rem(place[0] - k + NY, NY)) * 2
            for q in range(2):
                one = block[2 * q * rows:(2 * q + 1) * rows]
                two = block[(2 * q + 1) * rows:(2 * q + 2) * rows]
                first = place[3] == 0
                keep[at + q] = jnp.where(first, one, two)
                give[at + q] = jnp.where(first, two, one).astype(BF)


def row_terms(place, inner, grads):
    old, n = inner.shape[1], grads[0].shape[2]
    shape = (NX * NZ, n * ZH * NY // MP, old)
    return call(
        row_body, place, (inner, *grads), [struct(shape, F32), struct(shape, BF)],
        2 * inner.size * n * ZH * NY,
    )


def out_body(place, mixed, *refs):
    inner, out = refs[:NY], refs[NY]
    total = jnp.zeros(out.shape, F32)
    for k in range(NY):
        for h in range(ZH):
            rows = mixed[:, h, k]
            total += dot(inner[k][h], rows.reshape(-1, rows.shape[-1]), NN)
    out[...] = total.astype(out.dtype)


def grown_output(place, mixed, inner):
    hidden = inner[0].shape[1]
    return call(
        out_body, place, (mixed, *inner), struct((hidden, mixed.shape[-1]), BF),
        2 * mixed.size * hidden,
    )


def exchange_y(block_for):
    got = {k: lax.ppermute(block_for(k), "dp", shift_y(k)) for k in (2, 1, 3)}
    return [None, got[1], got[2], got[3]]


def sum_dp(blocks):
    got = exchange_y(lambda k: blocks[k])
    part = blocks[0] + got[1].astype(F32) + got[2].astype(F32) + got[3].astype(F32)
    return part + lax.ppermute(part.astype(BF), "dp", SWAP_ZH).astype(F32)


def gather_y(block):
    return [block] + exchange_y(lambda k: block)[1:]


def source_blocks(saved, slot_of, z_hi, y):
    width = saved.shape[1]
    sub = saved.shape[0] // (MP * NY)
    rows = saved.reshape(NC, NX, NZ, NY, sub, width)
    mine = pick(rows, y, 3).transpose(1, 2, 0, 3, 4).reshape(MP, sub, width)
    slots = lax.all_to_all(mine, "mp", 0, 0)
    panels = jnp.take(slots, slot_of, axis=0).reshape(ZH, NY, -1, sub, width)
    panels = pick(panels, z_hi)
    got = exchange_y(lambda k: pick(panels, (y + k) % NY))
    got[0] = pick(panels, y)
    chunk = jnp.stack([choose((y - j) % NY, got) for j in range(NY)])
    chunk = chunk.transpose(0, 2, 1, 3).reshape(NY * sub, -1)
    z = lax.axis_index("mp") // NC % NZ
    got = [chunk] + [lax.ppermute(chunk, "mp", flip_z(k)) for k in (1, 2, 3)]
    strip = jnp.concatenate([choose(z ^ j, got) for j in range(NZ)])
    got = {k: lax.ppermute(strip, "mp", shift_x(k)) for k in (2, 1, 3)}
    got[0] = strip
    blocks = []
    for k in range(NX):
        blocks += [got[k], lax.ppermute(got[k], "mp", SWAP_CORE)]
    return blocks


def mixed_strips(tokens, row_growth, z_hi, mp_index):
    old = row_growth.shape[1]
    strip = old // (NX * NZ)
    mine = pick(row_growth.T.reshape(NX * NZ, strip, -1), mp_index // NC)
    other = lax.ppermute(mine, "dp", SWAP_ZH)
    mine = jnp.where(z_hi == mp_index % NC, mine, other)
    strips = jnp.concatenate(gather_y(mine))
    mixed = dot(strips, tokens, NT).astype(BF)
    mixed = lax.all_gather(mixed, "mp", axis=0, tiled=True)
    return mixed.reshape(NX * NZ, NC, NY, strip, -1)


def shards(tokens, cotangent, saved_panels, owners, row_growth, col_growth):
    dp_index, mp_index = lax.axis_index("dp"), lax.axis_index("mp")
    z_hi, y = dp_index // NY, dp_index % NY
    x, core = mp_index // (NZ * NC), mp_index % NC
    place = jnp.stack([y, z_hi, x, core]).astype(jnp.int32)
    slot_of = owners[:, 1] * (MP // SECTIONS) + owners[:, 0]

    source = source_blocks(saved_panels, slot_of, z_hi, y)
    mixed = mixed_strips(tokens, row_growth, z_hi, mp_index)

    grads = sum_dp(grad_terms(place, tokens, cotangent.T))
    grad = pick(grads, z_hi).T
    grads = gather_y(grads.astype(BF))
    back = back_block(place, row_growth, grads)
    other = lax.ppermute(back, "dp", SWAP_ZH)
    pair = jnp.where(z_hi == 0, jnp.stack([back, other]), jnp.stack([other, back]))
    grad_col = col_grad(place, source, gather_y(pair))

    inners = sum_dp(inner_terms(place, col_growth, source)).astype(BF)
    keep, give = row_terms(place, pick(inners, z_hi), grads)
    keep = keep + lax.ppermute(give, "mp", SWAP_CORE).astype(F32)
    keep = lax.all_to_all(keep.astype(BF), "mp", 0, 0, axis_index_groups=PLANE_GROUPS)
    grad_row = keep.astype(F32).sum(axis=0)
    grown_out = grown_output(place, mixed, gather_y(inners)).T
    return (grown_out, grad, grad_row, grad_col)


def solution(mesh):
    in_specs = (P("dp", None), P("dp", "mp"), P(None, "mp"), P(), P(None, "dp"), P("mp", "dp"))
    out_specs = (P("dp", "mp"), P("dp", "mp"), P("mp", "dp"), P("mp", "dp"))
    return jax.shard_map(shards, mesh=mesh, in_specs=in_specs, out_specs=out_specs, check_vma=False)
```

```python
import jax
import jax.numpy as jnp
from jax import lax
from jax.experimental import pallas as pl
from jax.experimental.pallas import tpu as pltpu
from jax.sharding import PartitionSpec as P

SECTIONS = 4
ZH, NY = 2, 4
NX, NZ, NC = 4, 4, 2
MP = NX * NZ * NC
PLANE_GROUPS = [[(x * NZ + z) * NC + c for x in range(NX) for z in range(NZ)] for c in range(NC)]
SWAP_ZH = [(i, (i + NY) % (ZH * NY)) for i in range(ZH * NY)]
SWAP_CORE = [(m, m ^ 1) for m in range(MP)]
BF, F32 = jnp.bfloat16, jnp.float32
NN, NT, TN = ((1,), (0,)), ((1,), (1,)), ((0,), (0,))


def shift_y(k):
    return [(h * NY + y, h * NY + (y + k) % NY) for h in range(ZH) for y in range(NY)]


def shift_x(k):
    return [
        ((x * NZ + z) * NC + c, ((x + k) % NX * NZ + z) * NC + c)
        for x in range(NX) for z in range(NZ) for c in range(NC)
    ]


def flip_z(k):
    return [
        ((x * NZ + z) * NC + c, (x * NZ + (z ^ k)) * NC + c)
        for x in range(NX) for z in range(NZ) for c in range(NC)
    ]


def dot(a, b, dims):
    return lax.dot_general(a, b, (dims, ((), ())), preferred_element_type=F32)


def pick(blocks, index, axis=0):
    return lax.dynamic_index_in_dim(blocks, index, axis, keepdims=False)


def choose(index, cases):
    out = cases[-1]
    for at in range(len(cases) - 1):
        out = jnp.where(index == at, cases[at], out)
    return out


def call(body, place, arrays, outs, flops, scratch=(), grid=None, in_specs=None, out_specs=None):
    size = lambda s: s.size * s.dtype.itemsize
    whole = pl.BlockSpec(memory_space=pltpu.VMEM)
    return pl.pallas_call(
        body,
        out_shape=outs,
        grid=grid or (),
        in_specs=[pl.BlockSpec(memory_space=pltpu.SMEM)] + (in_specs or [whole] * len(arrays)),
        out_specs=out_specs or jax.tree.map(lambda _: whole, outs),
        scratch_shapes=list(scratch),
        compiler_params=pltpu.CompilerParams(vmem_limit_bytes=40 * 2**20),
        cost_estimate=pl.CostEstimate(
            flops=flops,
            bytes_accessed=sum(map(size, arrays)) + sum(map(size, jax.tree.leaves(outs))),
            transcendentals=0,
        ),
    )(place, *arrays)


def struct(shape, kind):
    return jax.ShapeDtypeStruct(shape, kind)


def put(value, k, at, outs):
    for case, out in enumerate(outs):
        @pl.when(k == case)
        def _():
            out[at] = value.astype(out.dtype)


def grad_body(place, tokens, cot, *outs):
    step = pl.program_id(0)
    both = dot(cot[...], tokens[...], NN)
    n = both.shape[1] // 2
    for half in range(2):
        block = 2 * step + half
        put(
            both[:, half * n:(half + 1) * n],
            lax.rem(lax.rem(block, NY) - place[0] + NY, NY),
            block // NY,
            outs,
        )


def grad_terms(place, tokens, cot):
    n = tokens.shape[1] // (ZH * NY)
    hidden = cot.shape[0]
    shape = (ZH, hidden, n)
    outs = [struct(shape, F32)] + [struct(shape, BF)] * (NY - 1)
    full = pl.BlockSpec(shape, lambda s: (0, 0, 0))
    return call(
        grad_body, place, (tokens, cot), outs, 2 * tokens.size * hidden,
        grid=(ZH * NY // 2,),
        in_specs=[
            pl.BlockSpec((tokens.shape[0], 2 * n), lambda s: (0, s)),
            pl.BlockSpec(cot.shape, lambda s: (0, 0)),
        ],
        out_specs=[full] * NY,
    )


def back_body(place, grown, *refs):
    grads, out = refs[:NY], refs[NY]
    n = grads[0].shape[2]
    total = jnp.zeros(out.shape, F32)
    for k in range(NY):
        for h in range(ZH):
            first = (h * NY + lax.rem(place[0] - k + NY, NY)) * n
            total += dot(grads[k][h], grown[pl.ds(pl.multiple_of(first, n), n), :], NN)
    out[...] = total.astype(out.dtype)


def back_block(place, row_growth, grads):
    hidden, old = grads[0].shape[1], row_growth.shape[1]
    return call(
        back_body, place, (row_growth, *grads), struct((hidden, old), BF),
        2 * row_growth.size * hidden,
    )


def inner_body(place, col, *refs):
    source, outs = refs[:2 * NX], refs[2 * NX:]
    for k in range(NX):
        for c in range(NC):
            block = dot(col[...], source[2 * k + c][...], NT)
            where = lax.rem(place[2] - k - place[0] + 2 * NX, NX)
            put(block, where, place[3] ^ c, outs)


def inner_terms(place, col, source):
    hidden, rows = col.shape[0], source[0].shape[0]
    shape = (ZH, hidden, rows)
    outs = [struct(shape, F32)] + [struct(shape, BF)] * (NY - 1)
    return call(inner_body, place, (col, *source), outs, 2 * col.size * rows * len(source))


def col_body(place, *refs):
    source, back, out, held = refs[:2 * NX], refs[2 * NX:2 * NX + NY], refs[-2], refs[-1]
    for k in range(NY):
        held[k] = back[k][...]
    total = jnp.zeros(out.shape, F32)
    for k in range(NX):
        for c in range(NC):
            at = lax.rem(place[0] - place[2] + k + NY, NY)
            total += dot(held[at, place[3] ^ c], source[2 * k + c][...], NN)
    out[...] = total


def col_grad(place, source, back):
    hidden, rows = back[0].shape[1:]
    return call(
        col_body, place, (*source, *back), struct((hidden, source[0].shape[1]), F32),
        2 * hidden * sum(s.size for s in source),
        scratch=[pltpu.VMEM((NY, *back[0].shape), BF)],
    )


def row_body(place, inner, *refs):
    grads, keep, give = refs[:NY], refs[NY], refs[NY + 1]
    rows = keep.shape[1]
    for k in range(NY):
        for h in range(ZH):
            block = dot(grads[k][h], inner[...], TN)
            at = (h * NY + lax.rem(place[0] - k + NY, NY)) * 2
            for q in range(2):
                one = block[2 * q * rows:(2 * q + 1) * rows]
                two = block[(2 * q + 1) * rows:(2 * q + 2) * rows]
                first = place[3] == 0
                keep[at + q] = jnp.where(first, one, two)
                give[at + q] = jnp.where(first, two, one).astype(BF)


def row_terms(place, inner, grads):
    old, n = inner.shape[1], grads[0].shape[2]
    shape = (NX * NZ, n * ZH * NY // MP, old)
    return call(
        row_body, place, (inner, *grads), [struct(shape, F32), struct(shape, BF)],
        2 * inner.size * n * ZH * NY,
    )


def out_body(place, mixed, *refs):
    inner, out = refs[:NY], refs[NY]
    total = jnp.zeros(out.shape, F32)
    for k in range(NY):
        for h in range(ZH):
            rows = mixed[:, h, k]
            total += dot(inner[k][h], rows.reshape(-1, rows.shape[-1]), NN)
    out[...] = total.astype(out.dtype)


def grown_output(place, mixed, inner):
    hidden = inner[0].shape[1]
    return call(
        out_body, place, (mixed, *inner), struct((hidden, mixed.shape[-1]), BF),
        2 * mixed.size * hidden,
    )


def after(value, *done):
    return lax.optimization_barrier((value, done))[0]


def exchange_y(block_for):
    got = {k: lax.ppermute(block_for(k), "dp", shift_y(k)) for k in (2, 1, 3)}
    return [None, got[1], got[2], got[3]]


def sum_y(blocks):
    got = exchange_y(lambda k: blocks[k])
    return blocks[0] + got[1].astype(F32) + got[2].astype(F32) + got[3].astype(F32)


def sum_z(part):
    return part + lax.ppermute(part.astype(BF), "dp", SWAP_ZH).astype(F32)


def gather_y(block):
    return [block] + exchange_y(lambda k: block)[1:]


def panel_slots(saved, y):
    width = saved.shape[1]
    sub = saved.shape[0] // (MP * NY)
    rows = saved.reshape(NC, NX, NZ, NY, sub, width)
    mine = pick(rows, y, 3).transpose(1, 2, 0, 3, 4).reshape(MP, sub, width)
    return lax.all_to_all(mine, "mp", 0, 0)


def panel_strip(slots, slot_of, z_hi, y):
    sub, width = slots.shape[1:]
    panels = jnp.take(slots, slot_of, axis=0).reshape(ZH, NY, -1, sub, width)
    panels = pick(panels, z_hi)
    got = exchange_y(lambda k: pick(panels, (y + k) % NY))
    got[0] = pick(panels, y)
    chunk = jnp.stack([choose((y - j) % NY, got) for j in range(NY)])
    chunk = chunk.transpose(0, 2, 1, 3).reshape(NY * sub, -1)
    z = lax.axis_index("mp") // NC % NZ
    got = [chunk] + [lax.ppermute(chunk, "mp", flip_z(k)) for k in (1, 2, 3)]
    return jnp.concatenate([choose(z ^ j, got) for j in range(NZ)])


def source_blocks(strip):
    got = {k: lax.ppermute(strip, "mp", shift_x(k)) for k in (2, 1, 3)}
    got[0] = strip
    blocks = []
    for k in range(NX):
        blocks += [got[k], lax.ppermute(got[k], "mp", SWAP_CORE)]
    return blocks


def mixed_strips(tokens, row_growth, z_hi, mp_index):
    old = row_growth.shape[1]
    strip = old // (NX * NZ)
    mine = pick(row_growth.T.reshape(NX * NZ, strip, -1), mp_index // NC)
    other = lax.ppermute(mine, "dp", SWAP_ZH)
    mine = jnp.where(z_hi == mp_index % NC, mine, other)
    strips = jnp.concatenate(gather_y(mine))
    return dot(strips, tokens, NT).astype(BF)


def shards(tokens, cotangent, saved_panels, owners, row_growth, col_growth):
    dp_index, mp_index = lax.axis_index("dp"), lax.axis_index("mp")
    z_hi, y = dp_index // NY, dp_index % NY
    x, core = mp_index // (NZ * NC), mp_index % NC
    place = jnp.stack([y, z_hi, x, core]).astype(jnp.int32)
    slot_of = owners[:, 1] * (MP // SECTIONS) + owners[:, 0]

    slots = panel_slots(saved_panels, y)
    terms = grad_terms(place, tokens, cotangent.T)
    mixed = mixed_strips(tokens, row_growth, z_hi, mp_index)
    mixed_all = lax.all_gather(mixed, "mp", axis=0, tiled=True)
    mixed_all = mixed_all.reshape(NX * NZ, NC, NY, -1, mixed.shape[1])

    strip = panel_strip(after(slots, terms), slot_of, z_hi, y)
    part = sum_y(terms)
    source = source_blocks(after(strip, part, mixed))

    grads = sum_z(part)
    grad = pick(grads, z_hi).T
    grads = gather_y(grads.astype(BF))
    back = back_block(place, row_growth, grads)

    other = lax.ppermute(back, "dp", SWAP_ZH)
    pair = jnp.where(z_hi == 0, jnp.stack([back, other]), jnp.stack([other, back]))
    backs = gather_y(pair)
    grad_col = col_grad(place, source, backs)

    inners = inner_terms(place, col_growth, after(source, grads))
    inners = sum_z(after(sum_y(inners), pair)).astype(BF)
    keep, give = row_terms(place, pick(inners, z_hi), grads)
    keep = keep + lax.ppermute(give, "mp", SWAP_CORE).astype(F32)
    keep = lax.all_to_all(keep.astype(BF), "mp", 0, 0, axis_index_groups=PLANE_GROUPS)
    grad_row = keep.astype(F32).sum(axis=0)
    grown_out = grown_output(place, mixed_all, gather_y(after(inners, backs))).T
    return (grown_out, grad, grad_row, grad_col)


def solution(mesh):
    in_specs = (P("dp", None), P("dp", "mp"), P(None, "mp"), P(), P(None, "dp"), P("mp", "dp"))
    out_specs = (P("dp", "mp"), P("dp", "mp"), P("mp", "dp"), P("mp", "dp"))
    return jax.shard_map(shards, mesh=mesh, in_specs=in_specs, out_specs=out_specs, check_vma=False)
```

```python
import jax
import jax.numpy as jnp
from jax import lax
from jax.experimental import pallas as pl
from jax.experimental.pallas import tpu as pltpu
from jax.sharding import PartitionSpec as P

SECTIONS = 4
ZH, NY = 2, 4
NX, NZ, NC = 4, 4, 2
MP = NX * NZ * NC
PLANE_GROUPS = [[(x * NZ + z) * NC + c for x in range(NX) for z in range(NZ)] for c in range(NC)]
SWAP_ZH = [(i, (i + NY) % (ZH * NY)) for i in range(ZH * NY)]
SWAP_CORE = [(m, m ^ 1) for m in range(MP)]
BF, F32 = jnp.bfloat16, jnp.float32
NN, NT, TN = ((1,), (0,)), ((1,), (1,)), ((0,), (0,))


def shift_y(k):
    return [(h * NY + y, h * NY + (y + k) % NY) for h in range(ZH) for y in range(NY)]


def dot(a, b, dims):
    return lax.dot_general(a, b, (dims, ((), ())), preferred_element_type=F32)


def pick(blocks, index, axis=0):
    return lax.dynamic_index_in_dim(blocks, index, axis, keepdims=False)


def choose(index, cases):
    out = cases[-1]
    for at in range(len(cases) - 1):
        out = jnp.where(index == at, cases[at], out)
    return out


def call(body, place, arrays, outs, flops, scratch=(), grid=None, in_specs=None, out_specs=None):
    size = lambda s: s.size * s.dtype.itemsize
    whole = pl.BlockSpec(memory_space=pltpu.VMEM)
    return pl.pallas_call(
        body,
        out_shape=outs,
        grid=grid or (),
        in_specs=[pl.BlockSpec(memory_space=pltpu.SMEM)] + (in_specs or [whole] * len(arrays)),
        out_specs=out_specs or jax.tree.map(lambda _: whole, outs),
        scratch_shapes=list(scratch),
        compiler_params=pltpu.CompilerParams(vmem_limit_bytes=40 * 2**20),
        cost_estimate=pl.CostEstimate(
            flops=flops,
            bytes_accessed=sum(map(size, arrays)) + sum(map(size, jax.tree.leaves(outs))),
            transcendentals=0,
        ),
    )(place, *arrays)


def struct(shape, kind):
    return jax.ShapeDtypeStruct(shape, kind)


def put(value, k, at, outs):
    for case, out in enumerate(outs):
        @pl.when(k == case)
        def _():
            out[at] = value.astype(out.dtype)


def grad_body(place, tokens, cot, *outs):
    step = pl.program_id(0)
    both = dot(cot[...], tokens[...], NN)
    n = both.shape[1] // 2
    for half in range(2):
        block = 2 * step + half
        put(
            both[:, half * n:(half + 1) * n],
            lax.rem(lax.rem(block, NY) - place[0] + NY, NY),
            block // NY,
            outs,
        )


def grad_terms(place, tokens, cot):
    n = tokens.shape[1] // (ZH * NY)
    hidden = cot.shape[0]
    shape = (ZH, hidden, n)
    outs = [struct(shape, F32)] + [struct(shape, BF)] * (NY - 1)
    full = pl.BlockSpec(shape, lambda s: (0, 0, 0))
    return call(
        grad_body, place, (tokens, cot), outs, 2 * tokens.size * hidden,
        grid=(ZH * NY // 2,),
        in_specs=[
            pl.BlockSpec((tokens.shape[0], 2 * n), lambda s: (0, s)),
            pl.BlockSpec(cot.shape, lambda s: (0, 0)),
        ],
        out_specs=[full] * NY,
    )


def back_body(place, grown, *refs):
    grads, out = refs[:NY], refs[NY]
    n = grads[0].shape[2]
    total = jnp.zeros(out.shape, F32)
    for k in range(NY):
        for h in range(ZH):
            first = (h * NY + lax.rem(place[0] - k + NY, NY)) * n
            total += dot(grads[k][h], grown[pl.ds(pl.multiple_of(first, n), n), :], NN)
    out[...] = total.astype(out.dtype)


def back_block(place, row_growth, grads):
    hidden, old = grads[0].shape[1], row_growth.shape[1]
    return call(
        back_body, place, (row_growth, *grads), struct((hidden, old), BF),
        2 * row_growth.size * hidden,
    )


def inner_body(place, col, mine, other, *outs):
    block = pl.program_id(0)
    k = lax.rem(block - place[0] + NY, NY)
    put(dot(col[...], mine[...], NT), k, place[3], outs)
    put(dot(col[...], other[...], NT), k, 1 - place[3], outs)


def stream(rows, width):
    return pl.BlockSpec((rows, width), lambda s: (s, 0))


def keep_whole(shape):
    return pl.BlockSpec(shape, lambda s: (0,) * len(shape))


def inner_terms(place, col, source):
    hidden, width = col.shape
    rows = source[0].shape[0] // NY
    shape = (ZH, hidden, rows)
    outs = [struct(shape, F32)] + [struct(shape, BF)] * (NY - 1)
    return call(
        inner_body, place, (col, *source), outs, 4 * source[0].size * hidden,
        grid=(NY,),
        in_specs=[keep_whole(col.shape), stream(rows, width), stream(rows, width)],
        out_specs=[keep_whole(shape)] * NY,
    )


def col_body(place, mine, other, *refs):
    back, out, held = refs[:NY], refs[NY], refs[NY + 1]
    block = pl.program_id(0)

    @pl.when(block == 0)
    def _():
        for k in range(NY):
            held[k] = back[k][...]
        out[...] = jnp.zeros(out.shape, F32)

    k = lax.rem(place[0] - block + NY, NY)
    out[...] += dot(held[k, place[3]], mine[...], NN) + dot(held[k, 1 - place[3]], other[...], NN)


def col_grad(place, source, back):
    hidden, rows = back[0].shape[1:]
    width = source[0].shape[1]
    return call(
        col_body, place, (*source, *back), struct((hidden, width), F32),
        4 * source[0].size * hidden,
        scratch=[pltpu.VMEM((NY, *back[0].shape), BF)],
        grid=(NY,),
        in_specs=[stream(rows, width)] * 2 + [keep_whole(back[0].shape)] * NY,
        out_specs=keep_whole((hidden, width)),
    )


def row_body(place, inner, *refs):
    grads, keep, give = refs[:NY], refs[NY], refs[NY + 1]
    rows = keep.shape[1]
    for k in range(NY):
        for h in range(ZH):
            block = dot(grads[k][h], inner[...], TN)
            at = (h * NY + lax.rem(place[0] - k + NY, NY)) * 2
            for q in range(2):
                one = block[2 * q * rows:(2 * q + 1) * rows]
                two = block[(2 * q + 1) * rows:(2 * q + 2) * rows]
                first = place[3] == 0
                keep[at + q] = jnp.where(first, one, two)
                give[at + q] = jnp.where(first, two, one).astype(BF)


def row_terms(place, inner, grads):
    old, n = inner.shape[1], grads[0].shape[2]
    shape = (NX * NZ, n * ZH * NY // MP, old)
    return call(
        row_body, place, (inner, *grads), [struct(shape, F32), struct(shape, BF)],
        2 * inner.size * n * ZH * NY,
    )


def out_body(place, mine, other, *refs):
    inner, out = refs[:NY], refs[NY]
    total = jnp.zeros(out.shape, F32)
    for k in range(NY):
        for rows, h in ((mine, place[3]), (other, 1 - place[3])):
            total += dot(inner[k][h], rows[:, k].reshape(-1, out.shape[1]), NN)
    out[...] = total.astype(out.dtype)


def grown_output(place, mixed, inner):
    hidden, count = inner[0].shape[1], mixed[0].shape[-1]
    part = count // 4
    rows = pl.BlockSpec((*mixed[0].shape[:-1], part), lambda s: (0, 0, 0, s))
    return call(
        out_body, place, (*mixed, *inner), struct((hidden, count), BF),
        4 * mixed[0].size * hidden,
        grid=(count // part,),
        in_specs=[rows] * 2 + [keep_whole(inner[0].shape)] * NY,
        out_specs=pl.BlockSpec((hidden, part), lambda s: (0, s)),
    )


def after(value, *done):
    return lax.optimization_barrier((value, done))[0]


def exchange_y(block_for):
    got = {k: lax.ppermute(block_for(k), "dp", shift_y(k)) for k in (2, 1, 3)}
    return [None, got[1], got[2], got[3]]


def sum_y(blocks):
    got = exchange_y(lambda k: blocks[k])
    return blocks[0] + got[1].astype(F32) + got[2].astype(F32) + got[3].astype(F32)


def sum_z(part):
    return part + lax.ppermute(part.astype(BF), "dp", SWAP_ZH).astype(F32)


def gather_y(block):
    return [block] + exchange_y(lambda k: block)[1:]


def panel_slots(saved, y):
    width = saved.shape[1]
    sub = saved.shape[0] // (MP * NY)
    rows = saved.reshape(NC, NX, NZ, NY, sub, width)
    mine = pick(rows, y, 3).transpose(1, 2, 0, 3, 4).reshape(MP, sub, width)
    return lax.all_to_all(mine, "mp", 0, 0)


def panel_rows(slots, slot_of, z_hi, y):
    sub, width = slots.shape[1:]
    panels = jnp.take(slots, slot_of, axis=0).reshape(ZH, NY, -1, sub, width)
    panels = pick(panels, z_hi)
    got = exchange_y(lambda k: pick(panels, (y + k) % NY))
    got[0] = pick(panels, y)
    chunk = jnp.stack([choose((y - j) % NY, got) for j in range(NY)])
    return chunk.transpose(0, 2, 1, 3).reshape(NY * sub, -1)


def gather_plane(block):
    return lax.all_gather(block, "mp", axis=0, tiled=True, axis_index_groups=PLANE_GROUPS)


def both_cores(half):
    return [half, lax.ppermute(half, "mp", SWAP_CORE)]


def mixed_strips(tokens, row_growth, z_hi, mp_index):
    old = row_growth.shape[1]
    strip = old // (NX * NZ)
    mine = pick(row_growth.T.reshape(NX * NZ, strip, -1), mp_index // NC)
    other = lax.ppermute(mine, "dp", SWAP_ZH)
    mine = jnp.where(z_hi == mp_index % NC, mine, other)
    strips = jnp.concatenate(gather_y(mine))
    return dot(strips, tokens, NT).astype(BF)


def shards(tokens, cotangent, saved_panels, owners, row_growth, col_growth):
    dp_index, mp_index = lax.axis_index("dp"), lax.axis_index("mp")
    z_hi, y = dp_index // NY, dp_index % NY
    x, core = mp_index // (NZ * NC), mp_index % NC
    place = jnp.stack([y, z_hi, x, core]).astype(jnp.int32)
    slot_of = owners[:, 1] * (MP // SECTIONS) + owners[:, 0]

    slots = panel_slots(saved_panels, y)
    terms = grad_terms(place, tokens, cotangent.T)
    mixed = mixed_strips(tokens, row_growth, z_hi, mp_index)

    half = gather_plane(panel_rows(after(slots, terms), slot_of, z_hi, y))
    grads = sum_z(sum_y(terms))
    half = after(half, grads, mixed)
    source = both_cores(half)

    mixed = gather_plane(after(mixed, half)).reshape(NX * NZ, NY, -1, mixed.shape[1])
    mixed = both_cores(mixed)

    grad = pick(grads, z_hi).T
    grads = gather_y(grads.astype(BF))
    back = back_block(place, row_growth, grads)

    other = lax.ppermute(back, "dp", SWAP_ZH)
    pair = jnp.where(z_hi == 0, jnp.stack([back, other]), jnp.stack([other, back]))
    backs = gather_y(pair)
    grad_col = col_grad(place, source, backs)

    inners = inner_terms(place, col_growth, source)
    inners = sum_z(after(sum_y(inners), pair)).astype(BF)
    keep, give = row_terms(place, pick(inners, z_hi), grads)
    keep = keep + lax.ppermute(give, "mp", SWAP_CORE).astype(F32)
    keep = lax.all_to_all(keep.astype(BF), "mp", 0, 0, axis_index_groups=PLANE_GROUPS)
    grad_row = keep.astype(F32).sum(axis=0)
    grown_out = grown_output(place, mixed, gather_y(after(inners, backs))).T
    return (grown_out, grad, grad_row, grad_col)


def solution(mesh):
    in_specs = (P("dp", None), P("dp", "mp"), P(None, "mp"), P(), P(None, "dp"), P("mp", "dp"))
    out_specs = (P("dp", "mp"), P("dp", "mp"), P("mp", "dp"), P("mp", "dp"))
    return jax.shard_map(shards, mesh=mesh, in_specs=in_specs, out_specs=out_specs, check_vma=False)
```

```python
import jax
import jax.numpy as jnp
from jax import lax
from jax.experimental import pallas as pl
from jax.experimental.pallas import tpu as pltpu
from jax.sharding import PartitionSpec as P

SECTIONS = 4
ZH, NY = 2, 4
NX, NZ, NC = 4, 4, 2
MP = NX * NZ * NC
PLANE_GROUPS = [[(x * NZ + z) * NC + c for x in range(NX) for z in range(NZ)] for c in range(NC)]
SWAP_ZH = [(i, (i + NY) % (ZH * NY)) for i in range(ZH * NY)]
SWAP_CORE = [(m, m ^ 1) for m in range(MP)]
BF, F32 = jnp.bfloat16, jnp.float32
NN, NT, TN = ((1,), (0,)), ((1,), (1,)), ((0,), (0,))


def shift_y(k):
    return [(h * NY + y, h * NY + (y + k) % NY) for h in range(ZH) for y in range(NY)]


def shift_x(k):
    return [
        ((x * NZ + z) * NC + c, ((x + k) % NX * NZ + z) * NC + c)
        for x in range(NX) for z in range(NZ) for c in range(NC)
    ]


def flip_z(k):
    return [
        ((x * NZ + z) * NC + c, (x * NZ + (z ^ k)) * NC + c)
        for x in range(NX) for z in range(NZ) for c in range(NC)
    ]


def dot(a, b, dims):
    return lax.dot_general(a, b, (dims, ((), ())), preferred_element_type=F32)


def pick(blocks, index, axis=0):
    return lax.dynamic_index_in_dim(blocks, index, axis, keepdims=False)


def choose(index, cases):
    out = cases[-1]
    for at in range(len(cases) - 1):
        out = jnp.where(index == at, cases[at], out)
    return out


def call(body, place, arrays, outs, flops, scratch=(), limit=40, **specs):
    size = lambda s: s.size * s.dtype.itemsize
    whole = pl.BlockSpec(memory_space=pltpu.VMEM)
    return pl.pallas_call(
        body,
        out_shape=outs,
        grid=specs.get("grid", ()),
        in_specs=[pl.BlockSpec(memory_space=pltpu.SMEM)] + specs.get("in_specs", [whole] * len(arrays)),
        out_specs=specs.get("out_specs", jax.tree.map(lambda _: whole, outs)),
        scratch_shapes=list(scratch),
        compiler_params=pltpu.CompilerParams(vmem_limit_bytes=limit * 2**20),
        cost_estimate=pl.CostEstimate(
            flops=flops,
            bytes_accessed=sum(map(size, arrays)) + sum(map(size, jax.tree.leaves(outs))),
            transcendentals=0,
        ),
    )(place, *arrays)


def struct(shape, kind):
    return jax.ShapeDtypeStruct(shape, kind)


def put(value, k, at, outs):
    for case, out in enumerate(outs):
        @pl.when(k == case)
        def _():
            out[at] = value.astype(out.dtype)


def grad_body(place, tokens, cot, *outs):
    step = pl.program_id(0)
    both = dot(cot[...], tokens[...], NN)
    n = both.shape[1] // 2
    for half in range(2):
        block = 2 * step + half
        put(
            both[:, half * n:(half + 1) * n],
            lax.rem(lax.rem(block, NY) - place[0] + NY, NY),
            block // NY,
            outs,
        )


def grad_terms(place, tokens, cot):
    n = tokens.shape[1] // (ZH * NY)
    hidden = cot.shape[0]
    shape = (ZH, hidden, n)
    outs = [struct(shape, F32)] + [struct(shape, BF)] * (NY - 1)
    full = pl.BlockSpec(shape, lambda s: (0, 0, 0))
    return call(
        grad_body, place, (tokens, cot), outs, 2 * tokens.size * hidden,
        grid=(ZH * NY // 2,),
        in_specs=[
            pl.BlockSpec((tokens.shape[0], 2 * n), lambda s: (0, s)),
            pl.BlockSpec(cot.shape, lambda s: (0, 0)),
        ],
        out_specs=[full] * NY,
    )


def back_body(place, grown, *refs):
    grads, out = refs[:NY], refs[NY]
    n = grads[0].shape[2]
    total = jnp.zeros(out.shape, F32)
    for k in range(NY):
        for h in range(ZH):
            first = (h * NY + lax.rem(place[0] - k + NY, NY)) * n
            total += dot(grads[k][h], grown[pl.ds(pl.multiple_of(first, n), n), :], NN)
    out[...] = total.astype(out.dtype)


def back_block(place, row_growth, grads):
    hidden, old = grads[0].shape[1], row_growth.shape[1]
    return call(
        back_body, place, (row_growth, *grads), struct((hidden, old), BF),
        2 * row_growth.size * hidden,
    )


def inner_body(place, col, *refs):
    source, outs = refs[:NC * NX], refs[NC * NX:]
    for c in range(NC):
        for k in range(NX):
            block = dot(col[...], source[c * NX + k][...], NT)
            at = lax.rem(place[2] - k - place[0] + 2 * NY, NY)
            put(block, at, place[3] ^ c, outs)


def inner_terms(place, col, source):
    hidden, rows = col.shape[0], source[0].shape[0]
    shape = (ZH, hidden, rows)
    outs = [struct(shape, F32)] + [struct(shape, BF)] * (NY - 1)
    return call(inner_body, place, (col, *source), outs, 2 * col.size * rows * len(source))


def col_body(place, *refs):
    source, back = refs[:NC * NX], refs[NC * NX:NC * NX + NY]
    out, held = refs[-2], refs[-1]
    for k in range(NY):
        held[k] = back[k][...]
    total = jnp.zeros(out.shape, F32)
    for c in range(NC):
        for k in range(NX):
            at = lax.rem(place[0] - place[2] + k + NY, NY)
            total += dot(held[at, place[3] ^ c], source[c * NX + k][...], NN)
    out[...] = total


def col_grad(place, source, back):
    hidden, rows = back[0].shape[1:]
    return call(
        col_body, place, (*source, *back), struct((hidden, source[0].shape[1]), F32),
        2 * hidden * sum(s.size for s in source),
        scratch=[pltpu.VMEM((NY, *back[0].shape), BF)],
        limit=56,
    )


def row_body(place, inner, *refs):
    grads, keep, give = refs[:NY], refs[NY], refs[NY + 1]
    rows = keep.shape[1]
    for k in range(NY):
        for h in range(ZH):
            block = dot(grads[k][h], inner[...], TN)
            at = (h * NY + lax.rem(place[0] - k + NY, NY)) * 2
            for q in range(2):
                one = block[2 * q * rows:(2 * q + 1) * rows]
                two = block[(2 * q + 1) * rows:(2 * q + 2) * rows]
                first = place[3] == 0
                keep[at + q] = jnp.where(first, one, two)
                give[at + q] = jnp.where(first, two, one).astype(BF)


def row_terms(place, inner, grads):
    old, n = inner.shape[1], grads[0].shape[2]
    shape = (NX * NZ, n * ZH * NY // MP, old)
    return call(
        row_body, place, (inner, *grads), [struct(shape, F32), struct(shape, BF)],
        2 * inner.size * n * ZH * NY,
    )


def out_body(place, *refs):
    mixed, inner = refs[:NC * NX], refs[NC * NX:NC * NX + NY]
    out, held = refs[-2], refs[-1]
    for c in range(NC):
        for j in range(NX):
            held[c, lax.rem(place[2] - j + NX, NX)] = mixed[c * NX + j][...]
    total = jnp.zeros(out.shape, F32)
    for k in range(NY):
        for c in range(NC):
            rows = held[c, :, :, k]
            total += dot(inner[k][place[3] ^ c], rows.reshape(-1, out.shape[1]), NN)
    out[...] = total.astype(out.dtype)


def grown_output(place, mixed, inner):
    hidden, count = inner[0].shape[1], mixed[0].shape[-1]
    part = count // 4
    block = (*mixed[0].shape[:-1], part)
    return call(
        out_body, place, (*mixed, *inner), struct((hidden, count), BF),
        2 * len(mixed) * mixed[0].size * hidden,
        grid=(count // part,),
        in_specs=[pl.BlockSpec(block, lambda s: (0, 0, 0, s))] * len(mixed)
        + [pl.BlockSpec(inner[0].shape, lambda s: (0, 0, 0))] * NY,
        out_specs=pl.BlockSpec((hidden, part), lambda s: (0, s)),
        scratch=[pltpu.VMEM((NC, NX, *block), BF)],
        limit=56,
    )


def after(value, *done):
    return lax.optimization_barrier((value, done))[0]


def exchange_y(block_for):
    got = {k: lax.ppermute(block_for(k), "dp", shift_y(k)) for k in (2, 1, 3)}
    return [None, got[1], got[2], got[3]]


def sum_y(blocks):
    got = exchange_y(lambda k: blocks[k])
    return blocks[0] + got[1].astype(F32) + got[2].astype(F32) + got[3].astype(F32)


def sum_z(part):
    return part + lax.ppermute(part.astype(BF), "dp", SWAP_ZH).astype(F32)


def gather_y(block):
    return [block] + exchange_y(lambda k: block)[1:]


def panel_slots(saved, y):
    width = saved.shape[1]
    sub = saved.shape[0] // (MP * NY)
    rows = saved.reshape(NC, NX, NZ, NY, sub, width)
    mine = pick(rows, y, 3).transpose(1, 2, 0, 3, 4).reshape(MP, sub, width)
    return lax.all_to_all(mine, "mp", 0, 0)


def panel_rows(slots, slot_of, z_hi, y):
    sub, width = slots.shape[1:]
    panels = jnp.take(slots, slot_of, axis=0).reshape(ZH, NY, -1, sub, width)
    panels = pick(panels, z_hi)
    got = exchange_y(lambda k: pick(panels, (y + k) % NY))
    got[0] = pick(panels, y)
    chunk = jnp.stack([choose((y - j) % NY, got) for j in range(NY)])
    return chunk.transpose(0, 2, 1, 3).reshape(NY * sub, -1)


def gather_z(block, mp_index):
    z = mp_index // NC % NZ
    got = [block] + [lax.ppermute(block, "mp", flip_z(k)) for k in (1, 2, 3)]
    return jnp.concatenate([choose(z ^ j, got) for j in range(NZ)])


def gather_x(block):
    got = {k: lax.ppermute(block, "mp", shift_x(k)) for k in (2, 1, 3)}
    return [block, got[1], got[2], got[3]]


def both_cores(blocks):
    return blocks + [lax.ppermute(b, "mp", SWAP_CORE) for b in blocks]


def mixed_strips(tokens, row_growth, z_hi, mp_index):
    old = row_growth.shape[1]
    strip = old // (NX * NZ)
    mine = pick(row_growth.T.reshape(NX * NZ, strip, -1), mp_index // NC)
    other = lax.ppermute(mine, "dp", SWAP_ZH)
    mine = jnp.where(z_hi == mp_index % NC, mine, other)
    strips = jnp.concatenate(gather_y(mine))
    return dot(strips, tokens, NT).astype(BF)


def shards(tokens, cotangent, saved_panels, owners, row_growth, col_growth):
    dp_index, mp_index = lax.axis_index("dp"), lax.axis_index("mp")
    z_hi, y = dp_index // NY, dp_index % NY
    x, core = mp_index // (NZ * NC), mp_index % NC
    place = jnp.stack([y, z_hi, x, core]).astype(jnp.int32)
    slot_of = owners[:, 1] * (MP // SECTIONS) + owners[:, 0]

    slots = panel_slots(saved_panels, y)
    terms = grad_terms(place, tokens, cotangent.T)
    mixed = mixed_strips(tokens, row_growth, z_hi, mp_index)

    rows = panel_rows(after(slots, terms), slot_of, z_hi, y)
    rows = gather_z(rows, mp_index)
    part = sum_y(terms)
    rows, part = lax.optimization_barrier((rows, part))
    source = gather_x(rows)
    grads = sum_z(part)
    source = both_cores(after(source, mixed))

    mixed = gather_z(after(mixed, source), mp_index)
    mixed = gather_x(mixed.reshape(NZ, NY, -1, mixed.shape[1]))
    mixed = both_cores(mixed)

    grad = pick(grads, z_hi).T
    grads = gather_y(grads.astype(BF))
    back = back_block(place, row_growth, grads)

    other = lax.ppermute(back, "dp", SWAP_ZH)
    pair = jnp.where(z_hi == 0, jnp.stack([back, other]), jnp.stack([other, back]))
    backs = gather_y(pair)
    grad_col = col_grad(place, source, backs)

    inners = inner_terms(place, col_growth, source)
    inners = sum_z(after(sum_y(inners), pair)).astype(BF)
    keep, give = row_terms(place, pick(inners, z_hi), grads)
    keep = keep + lax.ppermute(give, "mp", SWAP_CORE).astype(F32)
    keep = lax.all_to_all(keep.astype(BF), "mp", 0, 0, axis_index_groups=PLANE_GROUPS)
    grad_row = keep.astype(F32).sum(axis=0)
    grown_out = grown_output(place, mixed, gather_y(after(inners, grad_col))).T
    return (grown_out, grad, grad_row, grad_col)


def solution(mesh):
    in_specs = (P("dp", None), P("dp", "mp"), P(None, "mp"), P(), P(None, "dp"), P("mp", "dp"))
    out_specs = (P("dp", "mp"), P("dp", "mp"), P("mp", "dp"), P("mp", "dp"))
    return jax.shard_map(shards, mesh=mesh, in_specs=in_specs, out_specs=out_specs, check_vma=False)
```

```python
import jax
import jax.numpy as jnp
from jax import lax
from jax.experimental import pallas as pl
from jax.experimental.pallas import tpu as pltpu
from jax.sharding import PartitionSpec as P

SECTIONS = 4
ZH, NY = 2, 4
NX, NZ, NC = 4, 4, 2
MP = NX * NZ * NC
PLANE_GROUPS = [[(x * NZ + z) * NC + c for x in range(NX) for z in range(NZ)] for c in range(NC)]
SWAP_ZH = [(i, (i + NY) % (ZH * NY)) for i in range(ZH * NY)]
SWAP_CORE = [(m, m ^ 1) for m in range(MP)]
BF, F32 = jnp.bfloat16, jnp.float32
NN, NT, TN = ((1,), (0,)), ((1,), (1,)), ((0,), (0,))


def shift_y(k):
    return [(h * NY + y, h * NY + (y + k) % NY) for h in range(ZH) for y in range(NY)]


def shift_x(k):
    return [
        ((x * NZ + z) * NC + c, ((x + k) % NX * NZ + z) * NC + c)
        for x in range(NX) for z in range(NZ) for c in range(NC)
    ]


def flip_z(k):
    return [
        ((x * NZ + z) * NC + c, (x * NZ + (z ^ k)) * NC + c)
        for x in range(NX) for z in range(NZ) for c in range(NC)
    ]


def dot(a, b, dims):
    return lax.dot_general(a, b, (dims, ((), ())), preferred_element_type=F32)


def pick(blocks, index, axis=0):
    return lax.dynamic_index_in_dim(blocks, index, axis, keepdims=False)


def choose(index, cases):
    out = cases[-1]
    for at in range(len(cases) - 1):
        out = jnp.where(index == at, cases[at], out)
    return out


def call(body, place, arrays, outs, flops, scratch=(), limit=40, **specs):
    size = lambda s: s.size * s.dtype.itemsize
    whole = pl.BlockSpec(memory_space=pltpu.VMEM)
    return pl.pallas_call(
        body,
        out_shape=outs,
        grid=specs.get("grid", ()),
        in_specs=[pl.BlockSpec(memory_space=pltpu.SMEM)] + specs.get("in_specs", [whole] * len(arrays)),
        out_specs=specs.get("out_specs", jax.tree.map(lambda _: whole, outs)),
        scratch_shapes=list(scratch),
        compiler_params=pltpu.CompilerParams(vmem_limit_bytes=limit * 2**20),
        cost_estimate=pl.CostEstimate(
            flops=flops,
            bytes_accessed=sum(map(size, arrays)) + sum(map(size, jax.tree.leaves(outs))),
            transcendentals=0,
        ),
    )(place, *arrays)


def struct(shape, kind):
    return jax.ShapeDtypeStruct(shape, kind)


def put(value, k, at, outs):
    for case, out in enumerate(outs):
        @pl.when(k == case)
        def _():
            out[at] = value.astype(out.dtype)


def grad_body(place, tokens, cot, *outs):
    step = pl.program_id(0)
    both = dot(cot[...], tokens[...], NN)
    n = both.shape[1] // 2
    for half in range(2):
        block = 2 * step + half
        put(
            both[:, half * n:(half + 1) * n],
            lax.rem(lax.rem(block, NY) - place[0] + NY, NY),
            block // NY,
            outs,
        )


def grad_terms(place, tokens, cot):
    n = tokens.shape[1] // (ZH * NY)
    hidden = cot.shape[0]
    shape = (ZH, hidden, n)
    outs = [struct(shape, F32)] + [struct(shape, BF)] * (NY - 1)
    full = pl.BlockSpec(shape, lambda s: (0, 0, 0))
    return call(
        grad_body, place, (tokens, cot), outs, 2 * tokens.size * hidden,
        grid=(ZH * NY // 2,),
        in_specs=[
            pl.BlockSpec((tokens.shape[0], 2 * n), lambda s: (0, s)),
            pl.BlockSpec(cot.shape, lambda s: (0, 0)),
        ],
        out_specs=[full] * NY,
    )


def back_body(place, grown, *refs):
    grads, out = refs[:NY], refs[NY]
    n = grads[0].shape[2]
    total = jnp.zeros(out.shape, F32)
    for k in range(NY):
        for h in range(ZH):
            first = (h * NY + lax.rem(place[0] - k + NY, NY)) * n
            total += dot(grads[k][h], grown[pl.ds(pl.multiple_of(first, n), n), :], NN)
    out[...] = total.astype(out.dtype)


def back_block(place, row_growth, grads):
    hidden, old = grads[0].shape[1], row_growth.shape[1]
    return call(
        back_body, place, (row_growth, *grads), struct((hidden, old), BF),
        2 * row_growth.size * hidden,
    )


def inner_body(place, col, *refs):
    source, outs = refs[:NC * NX], refs[NC * NX:]
    for c in range(NC):
        for k in range(NX):
            block = dot(col[...], source[c * NX + k][...], NT)
            at = lax.rem(place[2] - k - place[0] + 2 * NY, NY)
            put(block, at, place[3] ^ c, outs)


def inner_terms(place, col, source):
    hidden, rows = col.shape[0], source[0].shape[0]
    shape = (ZH, hidden, rows)
    outs = [struct(shape, F32)] + [struct(shape, BF)] * (NY - 1)
    return call(inner_body, place, (col, *source), outs, 2 * col.size * rows * len(source))


def col_body(place, *refs):
    source, back = refs[:NC * NX], refs[NC * NX:NC * NX + NY]
    out, held = refs[-2], refs[-1]
    for k in range(NY):
        held[k] = back[k][...]
    total = jnp.zeros(out.shape, F32)
    for c in range(NC):
        for k in range(NX):
            at = lax.rem(place[0] - place[2] + k + NY, NY)
            total += dot(held[at, place[3] ^ c], source[c * NX + k][...], NN)
    out[...] = total


def col_grad(place, source, back):
    hidden, rows = back[0].shape[1:]
    return call(
        col_body, place, (*source, *back), struct((hidden, source[0].shape[1]), F32),
        2 * hidden * sum(s.size for s in source),
        scratch=[pltpu.VMEM((NY, *back[0].shape), BF)],
        limit=56,
    )


def row_body(place, inner, *refs):
    grads, keep, give = refs[:NY], refs[NY], refs[NY + 1]
    rows = keep.shape[1]
    for k in range(NY):
        for h in range(ZH):
            block = dot(grads[k][h], inner[...], TN)
            at = (h * NY + lax.rem(place[0] - k + NY, NY)) * 2
            for q in range(2):
                one = block[2 * q * rows:(2 * q + 1) * rows]
                two = block[(2 * q + 1) * rows:(2 * q + 2) * rows]
                first = place[3] == 0
                keep[at + q] = jnp.where(first, one, two)
                give[at + q] = jnp.where(first, two, one).astype(BF)


def row_terms(place, inner, grads):
    old, n = inner.shape[1], grads[0].shape[2]
    shape = (NX * NZ, n * ZH * NY // MP, old)
    return call(
        row_body, place, (inner, *grads), [struct(shape, F32), struct(shape, BF)],
        2 * inner.size * n * ZH * NY,
    )


def out_body(place, *refs):
    mixed, inner = refs[:NC * NX], refs[NC * NX:NC * NX + NY]
    out, held = refs[-2], refs[-1]
    for c in range(NC):
        for j in range(NX):
            held[c, lax.rem(place[2] - j + NX, NX)] = mixed[c * NX + j][...]
    total = jnp.zeros(out.shape, F32)
    for k in range(NY):
        for c in range(NC):
            rows = held[c, :, :, k]
            total += dot(inner[k][place[3] ^ c], rows.reshape(-1, out.shape[1]), NN)
    out[...] = total.astype(out.dtype)


def grown_output(place, mixed, inner):
    hidden, count = inner[0].shape[1], mixed[0].shape[-1]
    part = count // 4
    block = (*mixed[0].shape[:-1], part)
    return call(
        out_body, place, (*mixed, *inner), struct((hidden, count), BF),
        2 * len(mixed) * mixed[0].size * hidden,
        grid=(count // part,),
        in_specs=[pl.BlockSpec(block, lambda s: (0, 0, 0, s))] * len(mixed)
        + [pl.BlockSpec(inner[0].shape, lambda s: (0, 0, 0))] * NY,
        out_specs=pl.BlockSpec((hidden, part), lambda s: (0, s)),
        scratch=[pltpu.VMEM((NC, NX, *block), BF)],
        limit=56,
    )


def after(value, *done):
    return lax.optimization_barrier((value, done))[0]


def exchange_y(block_for):
    got = {k: lax.ppermute(block_for(k), "dp", shift_y(k)) for k in (2, 1, 3)}
    return [None, got[1], got[2], got[3]]


def sum_y(blocks):
    got = exchange_y(lambda k: blocks[k])
    return blocks[0] + got[1].astype(F32) + got[2].astype(F32) + got[3].astype(F32)


def sum_z(part):
    return part + lax.ppermute(part.astype(BF), "dp", SWAP_ZH).astype(F32)


def gather_y(block):
    return [block] + exchange_y(lambda k: block)[1:]


def panel_slots(saved, y):
    width = saved.shape[1]
    sub = saved.shape[0] // (MP * NY)
    rows = saved.reshape(NC, NX, NZ, NY, sub, width)
    mine = pick(rows, y, 3).transpose(1, 2, 0, 3, 4).reshape(MP, sub, width)
    return lax.all_to_all(mine, "mp", 0, 0)


def panel_rows(slots, slot_of, z_hi, y):
    sub, width = slots.shape[1:]
    panels = jnp.take(slots, slot_of, axis=0).reshape(ZH, NY, -1, sub, width)
    panels = pick(panels, z_hi)
    got = exchange_y(lambda k: pick(panels, (y + k) % NY))
    got[0] = pick(panels, y)
    chunk = jnp.stack([choose((y - j) % NY, got) for j in range(NY)])
    return chunk.transpose(0, 2, 1, 3).reshape(NY * sub, -1)


def gather_z(block, mp_index):
    z = mp_index // NC % NZ
    got = [block] + [lax.ppermute(block, "mp", flip_z(k)) for k in (1, 2, 3)]
    return jnp.concatenate([choose(z ^ j, got) for j in range(NZ)])


def gather_x(block):
    got = {k: lax.ppermute(block, "mp", shift_x(k)) for k in (2, 1, 3)}
    return [block, got[1], got[2], got[3]]


def both_cores(blocks):
    return blocks + [lax.ppermute(b, "mp", SWAP_CORE) for b in blocks]


def mixed_strips(tokens, row_growth, z_hi, mp_index, *done):
    old = row_growth.shape[1]
    strip = old // (NX * NZ)
    mine = pick(row_growth.T.reshape(NX * NZ, strip, -1), mp_index // NC)
    mine = after(mine, *done)
    other = lax.ppermute(mine, "dp", SWAP_ZH)
    mine = jnp.where(z_hi == mp_index % NC, mine, other)
    strips = jnp.concatenate(gather_y(mine))
    return dot(strips, tokens, NT).astype(BF)


def shards(tokens, cotangent, saved_panels, owners, row_growth, col_growth):
    dp_index, mp_index = lax.axis_index("dp"), lax.axis_index("mp")
    z_hi, y = dp_index // NY, dp_index % NY
    x, core = mp_index // (NZ * NC), mp_index % NC
    place = jnp.stack([y, z_hi, x, core]).astype(jnp.int32)
    slot_of = owners[:, 1] * (MP // SECTIONS) + owners[:, 0]

    slots = panel_slots(saved_panels, y)
    terms = grad_terms(place, tokens, cotangent.T)
    rows = panel_rows(after(slots, terms), slot_of, z_hi, y)
    terms = after(terms, rows)
    rows = gather_z(rows, mp_index)
    part = sum_y(terms)
    source = gather_x(after(rows, part))
    grads = sum_z(part)
    mixed = mixed_strips(tokens, row_growth, z_hi, mp_index, part)
    source = both_cores(after(source, mixed))
    mixed = gather_z(mixed, mp_index)

    grad = pick(grads, z_hi).T
    grads = gather_y(grads.astype(BF))
    back = back_block(place, row_growth, grads)
    other = lax.ppermute(back, "dp", SWAP_ZH)
    pair = jnp.where(z_hi == 0, jnp.stack([back, other]), jnp.stack([other, back]))

    inners = after(inner_terms(place, col_growth, source), grads)
    part = after(sum_y(inners), pair, mixed)
    mixed = gather_x(mixed.reshape(NZ, NY, -1, mixed.shape[1]))
    mixed = both_cores(mixed)
    inners = sum_z(part).astype(BF)
    backs = gather_y(pair)
    grad_col = col_grad(place, source, backs)

    keep, give = row_terms(place, pick(inners, z_hi), grads)
    keep = keep + lax.ppermute(give, "mp", SWAP_CORE).astype(F32)
    keep = lax.all_to_all(keep.astype(BF), "mp", 0, 0, axis_index_groups=PLANE_GROUPS)
    grad_row = keep.astype(F32).sum(axis=0)
    inners = gather_y(after(inners, backs, mixed))
    grown_out = grown_output(place, after(mixed, grad_col, grad_row), inners).T
    return (grown_out, grad, grad_row, grad_col)


def solution(mesh):
    in_specs = (P("dp", None), P("dp", "mp"), P(None, "mp"), P(), P(None, "dp"), P("mp", "dp"))
    out_specs = (P("dp", "mp"), P("dp", "mp"), P("mp", "dp"), P("mp", "dp"))
    return jax.shard_map(shards, mesh=mesh, in_specs=in_specs, out_specs=out_specs, check_vma=False)
```

```python
import jax
import jax.numpy as jnp
from jax import lax
from jax.experimental import pallas as pl
from jax.experimental.pallas import tpu as pltpu
from jax.sharding import PartitionSpec as P

SECTIONS = 4
ZH, NY = 2, 4
NX, NZ, NC = 4, 4, 2
MP = NX * NZ * NC
PLANE_GROUPS = [[(x * NZ + z) * NC + c for x in range(NX) for z in range(NZ)] for c in range(NC)]
X_GROUPS = [[(x * NZ + z) * NC + c for x in range(NX)] for z in range(NZ) for c in range(NC)]
Z_GROUPS = [[(x * NZ + z) * NC + c for z in range(NZ)] for x in range(NX) for c in range(NC)]
SWAP_ZH = [(i, (i + NY) % (ZH * NY)) for i in range(ZH * NY)]
SWAP_CORE = [(m, m ^ 1) for m in range(MP)]
BF, F32 = jnp.bfloat16, jnp.float32
NN, NT, TN = ((1,), (0,)), ((1,), (1,)), ((0,), (0,))


def shift_y(k):
    return [(h * NY + y, h * NY + (y + k) % NY) for h in range(ZH) for y in range(NY)]


def dot(a, b, dims):
    return lax.dot_general(a, b, (dims, ((), ())), preferred_element_type=F32)


def pick(blocks, index, axis=0):
    return lax.dynamic_index_in_dim(blocks, index, axis, keepdims=False)


def choose(index, cases):
    out = cases[-1]
    for at in range(len(cases) - 1):
        out = jnp.where(index == at, cases[at], out)
    return out


def call(body, place, arrays, outs, flops, scratch=(), limit=40, **specs):
    size = lambda s: s.size * s.dtype.itemsize
    whole = pl.BlockSpec(memory_space=pltpu.VMEM)
    return pl.pallas_call(
        body,
        out_shape=outs,
        grid=specs.get("grid", ()),
        in_specs=[pl.BlockSpec(memory_space=pltpu.SMEM)] + specs.get("in_specs", [whole] * len(arrays)),
        out_specs=specs.get("out_specs", jax.tree.map(lambda _: whole, outs)),
        scratch_shapes=list(scratch),
        compiler_params=pltpu.CompilerParams(vmem_limit_bytes=limit * 2**20),
        cost_estimate=pl.CostEstimate(
            flops=flops,
            bytes_accessed=sum(map(size, arrays)) + sum(map(size, jax.tree.leaves(outs))),
            transcendentals=0,
        ),
    )(place, *arrays)


def struct(shape, kind):
    return jax.ShapeDtypeStruct(shape, kind)


def put(value, k, at, outs):
    for case, out in enumerate(outs):
        @pl.when(k == case)
        def _():
            out[at] = value.astype(out.dtype)


def grad_body(place, tokens, cot, *outs):
    step = pl.program_id(0)
    both = dot(cot[...], tokens[...], NN)
    n = both.shape[1] // 2
    for half in range(2):
        block = 2 * step + half
        put(
            both[:, half * n:(half + 1) * n],
            lax.rem(lax.rem(block, NY) - place[0] + NY, NY),
            block // NY,
            outs,
        )


def grad_terms(place, tokens, cot):
    n = tokens.shape[1] // (ZH * NY)
    hidden = cot.shape[0]
    shape = (ZH, hidden, n)
    outs = [struct(shape, F32)] + [struct(shape, BF)] * (NY - 1)
    full = pl.BlockSpec(shape, lambda s: (0, 0, 0))
    return call(
        grad_body, place, (tokens, cot), outs, 2 * tokens.size * hidden,
        grid=(ZH * NY // 2,),
        in_specs=[
            pl.BlockSpec((tokens.shape[0], 2 * n), lambda s: (0, s)),
            pl.BlockSpec(cot.shape, lambda s: (0, 0)),
        ],
        out_specs=[full] * NY,
    )


def back_body(place, grown, *refs):
    grads, out = refs[:NY], refs[NY]
    n = grads[0].shape[2]
    total = jnp.zeros(out.shape, F32)
    for k in range(NY):
        for h in range(ZH):
            first = (h * NY + lax.rem(place[0] - k + NY, NY)) * n
            total += dot(grads[k][h], grown[pl.ds(pl.multiple_of(first, n), n), :], NN)
    out[...] = total.astype(out.dtype)


def back_block(place, row_growth, grads):
    hidden, old = grads[0].shape[1], row_growth.shape[1]
    return call(
        back_body, place, (row_growth, *grads), struct((hidden, old), BF),
        2 * row_growth.size * hidden,
    )


def inner_body(place, col, mine, other, *outs):
    block = pl.program_id(0)
    k = lax.rem(block - place[0] + NY, NY)
    put(dot(col[...], mine[...], NT), k, place[3], outs)
    put(dot(col[...], other[...], NT), k, 1 - place[3], outs)


def stream(rows, width):
    return pl.BlockSpec((rows, width), lambda s: (s, 0))


def keep_whole(shape):
    return pl.BlockSpec(shape, lambda s: (0,) * len(shape))


def inner_terms(place, col, source):
    hidden, width = col.shape
    rows = source[0].shape[0] // NY
    shape = (ZH, hidden, rows)
    outs = [struct(shape, F32)] + [struct(shape, BF)] * (NY - 1)
    return call(
        inner_body, place, (col, *source), outs, 4 * source[0].size * hidden,
        grid=(NY,),
        in_specs=[keep_whole(col.shape), stream(rows, width), stream(rows, width)],
        out_specs=[keep_whole(shape)] * NY,
    )


def col_body(place, mine, other, *refs):
    back, out, held = refs[:NY], refs[NY], refs[NY + 1]
    block = pl.program_id(0)

    @pl.when(block == 0)
    def _():
        for k in range(NY):
            held[k] = back[k][...]
        out[...] = jnp.zeros(out.shape, F32)

    k = lax.rem(place[0] - block + NY, NY)
    out[...] += dot(held[k, place[3]], mine[...], NN) + dot(held[k, 1 - place[3]], other[...], NN)


def col_grad(place, source, back):
    hidden, rows = back[0].shape[1:]
    width = source[0].shape[1]
    return call(
        col_body, place, (*source, *back), struct((hidden, width), F32),
        4 * source[0].size * hidden,
        scratch=[pltpu.VMEM((NY, *back[0].shape), BF)],
        limit=56,
        grid=(NY,),
        in_specs=[stream(rows, width)] * 2 + [keep_whole(back[0].shape)] * NY,
        out_specs=keep_whole((hidden, width)),
    )


def row_body(place, inner, *refs):
    grads, keep, give = refs[:NY], refs[NY], refs[NY + 1]
    rows = keep.shape[1]
    for k in range(NY):
        for h in range(ZH):
            block = dot(grads[k][h], inner[...], TN)
            at = (h * NY + lax.rem(place[0] - k + NY, NY)) * 2
            for q in range(2):
                one = block[2 * q * rows:(2 * q + 1) * rows]
                two = block[(2 * q + 1) * rows:(2 * q + 2) * rows]
                first = place[3] == 0
                keep[at + q] = jnp.where(first, one, two)
                give[at + q] = jnp.where(first, two, one).astype(BF)


def row_terms(place, inner, grads):
    old, n = inner.shape[1], grads[0].shape[2]
    shape = (NX * NZ, n * ZH * NY // MP, old)
    return call(
        row_body, place, (inner, *grads), [struct(shape, F32), struct(shape, BF)],
        2 * inner.size * n * ZH * NY,
    )


def out_body(place, mine, other, *refs):
    inner, out = refs[:NY], refs[NY]
    total = jnp.zeros(out.shape, F32)
    for k in range(NY):
        for rows, h in ((mine, place[3]), (other, 1 - place[3])):
            total += dot(inner[k][h], rows[:, k].reshape(-1, out.shape[1]), NN)
    out[...] = total.astype(out.dtype)


def grown_output(place, mixed, inner):
    hidden, count = inner[0].shape[1], mixed[0].shape[-1]
    part = count // 4
    rows = pl.BlockSpec((*mixed[0].shape[:-1], part), lambda s: (0, 0, 0, s))
    return call(
        out_body, place, (*mixed, *inner), struct((hidden, count), BF),
        4 * mixed[0].size * hidden,
        limit=56,
        grid=(count // part,),
        in_specs=[rows] * 2 + [keep_whole(inner[0].shape)] * NY,
        out_specs=pl.BlockSpec((hidden, part), lambda s: (0, s)),
    )


def after(value, *done):
    return lax.optimization_barrier((value, done))[0]


def exchange_y(block_for):
    got = {k: lax.ppermute(block_for(k), "dp", shift_y(k)) for k in (2, 1, 3)}
    return [None, got[1], got[2], got[3]]


def sum_y(blocks):
    got = exchange_y(lambda k: blocks[k])
    return blocks[0] + got[1].astype(F32) + got[2].astype(F32) + got[3].astype(F32)


def sum_z(part):
    return part + lax.ppermute(part.astype(BF), "dp", SWAP_ZH).astype(F32)


def gather_y(block):
    return [block] + exchange_y(lambda k: block)[1:]


def panel_slots(saved, y):
    width = saved.shape[1]
    sub = saved.shape[0] // (MP * NY)
    rows = saved.reshape(NC, NX, NZ, NY, sub, width)
    mine = pick(rows, y, 3).transpose(1, 2, 0, 3, 4).reshape(MP, sub, width)
    return lax.all_to_all(mine, "mp", 0, 0)


def panel_rows(slots, slot_of, z_hi, y):
    sub, width = slots.shape[1:]
    panels = jnp.take(slots, slot_of, axis=0).reshape(ZH, NY, -1, sub, width)
    panels = pick(panels, z_hi)
    got = exchange_y(lambda k: pick(panels, (y + k) % NY))
    got[0] = pick(panels, y)
    chunk = jnp.stack([choose((y - j) % NY, got) for j in range(NY)])
    return chunk.transpose(0, 2, 1, 3).reshape(NY * sub, -1)


def gather(block, groups):
    blocks = jnp.broadcast_to(block[None], (len(groups[0]), *block.shape))
    return lax.all_to_all(blocks, "mp", 0, 0, axis_index_groups=groups).reshape(-1, *block.shape[1:])


def both_cores(half):
    return [half, lax.ppermute(half, "mp", SWAP_CORE)]


def mixed_strips(tokens, row_growth, z_hi, mp_index, *done):
    old = row_growth.shape[1]
    strip = old // (NX * NZ)
    mine = pick(row_growth.T.reshape(NX * NZ, strip, -1), mp_index // NC)
    mine = after(mine, *done)
    other = lax.ppermute(mine, "dp", SWAP_ZH)
    mine = jnp.where(z_hi == mp_index % NC, mine, other)
    strips = jnp.concatenate(gather_y(mine))
    return dot(strips, tokens, NT).astype(BF)


def shards(tokens, cotangent, saved_panels, owners, row_growth, col_growth):
    dp_index, mp_index = lax.axis_index("dp"), lax.axis_index("mp")
    z_hi, y = dp_index // NY, dp_index % NY
    x, core = mp_index // (NZ * NC), mp_index % NC
    place = jnp.stack([y, z_hi, x, core]).astype(jnp.int32)
    slot_of = owners[:, 1] * (MP // SECTIONS) + owners[:, 0]

    slots = panel_slots(saved_panels, y)
    terms = grad_terms(place, tokens, cotangent.T)
    rows = panel_rows(after(slots, terms), slot_of, z_hi, y)
    terms = after(terms, rows)
    half = gather(gather(rows, Z_GROUPS), X_GROUPS)
    source = both_cores(half)

    part = sum_y(terms)
    grads = sum_z(part)
    mixed = mixed_strips(tokens, row_growth, z_hi, mp_index, part)
    grad = pick(grads, z_hi).T
    grads = gather_y(grads.astype(BF))
    back = back_block(place, row_growth, grads)
    other = lax.ppermute(back, "dp", SWAP_ZH)
    pair = jnp.where(z_hi == 0, jnp.stack([back, other]), jnp.stack([other, back]))

    mixed = gather(after(mixed, half), Z_GROUPS)
    inners = inner_terms(place, col_growth, source)
    part = after(sum_y(inners), pair, mixed)
    mixed = gather(mixed, X_GROUPS).reshape(NX * NZ, NY, -1, mixed.shape[1])
    mixed = both_cores(mixed)
    inners = sum_z(part).astype(BF)
    backs = gather_y(pair)
    grad_col = col_grad(place, source, backs)

    keep, give = row_terms(place, pick(inners, z_hi), grads)
    keep = keep + lax.ppermute(give, "mp", SWAP_CORE).astype(F32)
    keep = lax.all_to_all(keep.astype(BF), "mp", 0, 0, axis_index_groups=PLANE_GROUPS)
    grad_row = keep.astype(F32).sum(axis=0)
    inners = gather_y(after(inners, backs, mixed))
    grown_out = grown_output(place, after(mixed, grad_col, grad_row), inners).T
    return (grown_out, grad, grad_row, grad_col)


def solution(mesh):
    in_specs = (P("dp", None), P("dp", "mp"), P(None, "mp"), P(), P(None, "dp"), P("mp", "dp"))
    out_specs = (P("dp", "mp"), P("dp", "mp"), P("mp", "dp"), P("mp", "dp"))
    return jax.shard_map(shards, mesh=mesh, in_specs=in_specs, out_specs=out_specs, check_vma=False)
```

```python
import jax
import jax.numpy as jnp
from jax import lax
from jax.experimental import pallas as pl
from jax.experimental.pallas import tpu as pltpu
from jax.sharding import PartitionSpec as P

SECTIONS = 4
ZH, NY = 2, 4
NX, NZ, NC = 4, 4, 2
MP = NX * NZ * NC
PLANE_GROUPS = [[(x * NZ + z) * NC + c for x in range(NX) for z in range(NZ)] for c in range(NC)]
X_GROUPS = [[(x * NZ + z) * NC + c for x in range(NX)] for z in range(NZ) for c in range(NC)]
Z_GROUPS = [[(x * NZ + z) * NC + c for z in range(NZ)] for x in range(NX) for c in range(NC)]
SWAP_ZH = [(i, (i + NY) % (ZH * NY)) for i in range(ZH * NY)]
SWAP_CORE = [(m, m ^ 1) for m in range(MP)]
BF, F32 = jnp.bfloat16, jnp.float32
NN, NT, TN = ((1,), (0,)), ((1,), (1,)), ((0,), (0,))


def shift_y(k):
    return [(h * NY + y, h * NY + (y + k) % NY) for h in range(ZH) for y in range(NY)]


def dot(a, b, dims):
    return lax.dot_general(a, b, (dims, ((), ())), preferred_element_type=F32)


def pick(blocks, index, axis=0):
    return lax.dynamic_index_in_dim(blocks, index, axis, keepdims=False)


def choose(index, cases):
    out = cases[-1]
    for at in range(len(cases) - 1):
        out = jnp.where(index == at, cases[at], out)
    return out


def call(body, place, arrays, outs, flops, scratch=(), limit=40, **specs):
    size = lambda s: s.size * s.dtype.itemsize
    whole = pl.BlockSpec(memory_space=pltpu.VMEM)
    return pl.pallas_call(
        body,
        out_shape=outs,
        grid=specs.get("grid", ()),
        in_specs=[pl.BlockSpec(memory_space=pltpu.SMEM)] + specs.get("in_specs", [whole] * len(arrays)),
        out_specs=specs.get("out_specs", jax.tree.map(lambda _: whole, outs)),
        scratch_shapes=list(scratch),
        compiler_params=pltpu.CompilerParams(vmem_limit_bytes=limit * 2**20),
        cost_estimate=pl.CostEstimate(
            flops=flops,
            bytes_accessed=sum(map(size, arrays)) + sum(map(size, jax.tree.leaves(outs))),
            transcendentals=0,
        ),
    )(place, *arrays)


def struct(shape, kind):
    return jax.ShapeDtypeStruct(shape, kind)


def put(value, k, at, outs):
    for case, out in enumerate(outs):
        @pl.when(k == case)
        def _():
            out[at] = value.astype(out.dtype)


def grad_body(place, tokens, cot, *outs):
    step = pl.program_id(0)
    both = dot(cot[...], tokens[...], NN)
    n = both.shape[1] // 2
    for half in range(2):
        block = 2 * step + half
        put(
            both[:, half * n:(half + 1) * n],
            lax.rem(lax.rem(block, NY) - place[0] + NY, NY),
            block // NY,
            outs,
        )


def grad_terms(place, tokens, cot):
    n = tokens.shape[1] // (ZH * NY)
    hidden = cot.shape[0]
    shape = (ZH, hidden, n)
    outs = [struct(shape, F32)] + [struct(shape, BF)] * (NY - 1)
    full = pl.BlockSpec(shape, lambda s: (0, 0, 0))
    return call(
        grad_body, place, (tokens, cot), outs, 2 * tokens.size * hidden,
        grid=(ZH * NY // 2,),
        in_specs=[
            pl.BlockSpec((tokens.shape[0], 2 * n), lambda s: (0, s)),
            pl.BlockSpec(cot.shape, lambda s: (0, 0)),
        ],
        out_specs=[full] * NY,
    )


def back_body(place, grown, *refs):
    grads, out = refs[:NY], refs[NY]
    n = grads[0].shape[2]
    total = jnp.zeros(out.shape, F32)
    for k in range(NY):
        for h in range(ZH):
            first = (h * NY + lax.rem(place[0] - k + NY, NY)) * n
            total += dot(grads[k][h], grown[pl.ds(pl.multiple_of(first, n), n), :], NN)
    out[...] = total.astype(out.dtype)


def back_block(place, row_growth, grads):
    hidden, old = grads[0].shape[1], row_growth.shape[1]
    return call(
        back_body, place, (row_growth, *grads), struct((hidden, old), BF),
        2 * row_growth.size * hidden,
    )


def inner_body(place, col, mine, other, *outs):
    block = pl.program_id(0)
    k = lax.rem(block - place[0] + NY, NY)
    put(dot(col[...], mine[...], NT), k, place[3], outs)
    put(dot(col[...], other[...], NT), k, 1 - place[3], outs)


def stream(rows, width):
    return pl.BlockSpec((rows, width), lambda s: (s, 0))


def keep_whole(shape):
    return pl.BlockSpec(shape, lambda s: (0,) * len(shape))


def inner_terms(place, col, source):
    hidden, width = col.shape
    rows = source[0].shape[0] // NY
    shape = (ZH, hidden, rows)
    outs = [struct(shape, F32)] + [struct(shape, BF)] * (NY - 1)
    return call(
        inner_body, place, (col, *source), outs, 4 * source[0].size * hidden,
        grid=(NY,),
        in_specs=[keep_whole(col.shape), stream(rows, width), stream(rows, width)],
        out_specs=[keep_whole(shape)] * NY,
    )


def col_body(place, mine, other, *refs):
    back, out, held = refs[:NY], refs[NY], refs[NY + 1]
    block = pl.program_id(0)

    @pl.when(block == 0)
    def _():
        for k in range(NY):
            held[k] = back[k][...]
        out[...] = jnp.zeros(out.shape, F32)

    k = lax.rem(place[0] - block + NY, NY)
    out[...] += dot(held[k, place[3]], mine[...], NN) + dot(held[k, 1 - place[3]], other[...], NN)


def col_grad(place, source, back):
    hidden, rows = back[0].shape[1:]
    width = source[0].shape[1]
    return call(
        col_body, place, (*source, *back), struct((hidden, width), F32),
        4 * source[0].size * hidden,
        scratch=[pltpu.VMEM((NY, *back[0].shape), BF)],
        limit=56,
        grid=(NY,),
        in_specs=[stream(rows, width)] * 2 + [keep_whole(back[0].shape)] * NY,
        out_specs=keep_whole((hidden, width)),
    )


def row_body(place, inner, *refs):
    grads, keep, give = refs[:NY], refs[NY], refs[NY + 1]
    rows = keep.shape[1]
    for k in range(NY):
        for h in range(ZH):
            block = dot(grads[k][h], inner[...], TN)
            at = (h * NY + lax.rem(place[0] - k + NY, NY)) * 2
            for q in range(2):
                one = block[2 * q * rows:(2 * q + 1) * rows]
                two = block[(2 * q + 1) * rows:(2 * q + 2) * rows]
                first = place[3] == 0
                keep[at + q] = jnp.where(first, one, two)
                give[at + q] = jnp.where(first, two, one).astype(BF)


def row_terms(place, inner, grads):
    old, n = inner.shape[1], grads[0].shape[2]
    shape = (NX * NZ, n * ZH * NY // MP, old)
    return call(
        row_body, place, (inner, *grads), [struct(shape, F32), struct(shape, BF)],
        2 * inner.size * n * ZH * NY,
    )


def out_body(place, mine, other, *refs):
    inner, out = refs[:NY], refs[NY]
    total = jnp.zeros(out.shape, F32)
    for k in range(NY):
        for rows, h in ((mine, place[3]), (other, 1 - place[3])):
            total += dot(inner[k][h], rows[:, k].reshape(-1, out.shape[1]), NN)
    out[...] = total.astype(out.dtype)


def grown_output(place, mixed, inner):
    hidden, count = inner[0].shape[1], mixed[0].shape[-1]
    part = count // 4
    rows = pl.BlockSpec((*mixed[0].shape[:-1], part), lambda s: (0, 0, 0, s))
    return call(
        out_body, place, (*mixed, *inner), struct((hidden, count), BF),
        4 * mixed[0].size * hidden,
        limit=56,
        grid=(count // part,),
        in_specs=[rows] * 2 + [keep_whole(inner[0].shape)] * NY,
        out_specs=pl.BlockSpec((hidden, part), lambda s: (0, s)),
    )


def together(*values):
    return lax.optimization_barrier(values)


def exchange_y(block_for):
    got = {k: lax.ppermute(block_for(k), "dp", shift_y(k)) for k in (2, 1, 3)}
    return [None, got[1], got[2], got[3]]


def sum_y(blocks):
    got = exchange_y(lambda k: blocks[k])
    return blocks[0] + got[1].astype(F32) + got[2].astype(F32) + got[3].astype(F32)


def sum_z(part):
    return part + lax.ppermute(part.astype(BF), "dp", SWAP_ZH).astype(F32)


def gather_y(block):
    return [block] + exchange_y(lambda k: block)[1:]


def panel_slots(saved, y):
    width = saved.shape[1]
    sub = saved.shape[0] // (MP * NY)
    rows = saved.reshape(NC, NX, NZ, NY, sub, width)
    mine = pick(rows, y, 3).transpose(1, 2, 0, 3, 4).reshape(MP, sub, width)
    return lax.all_to_all(mine, "mp", 0, 0)


def panel_rows(slots, slot_of, z_hi, y):
    sub, width = slots.shape[1:]
    panels = jnp.take(slots, slot_of, axis=0).reshape(ZH, NY, -1, sub, width)
    panels = pick(panels, z_hi)
    got = exchange_y(lambda k: pick(panels, (y + k) % NY))
    got[0] = pick(panels, y)
    chunk = jnp.stack([choose((y - j) % NY, got) for j in range(NY)])
    return chunk.transpose(0, 2, 1, 3).reshape(NY * sub, -1)


def gather(block, groups):
    blocks = jnp.broadcast_to(block[None], (len(groups[0]), *block.shape))
    return lax.all_to_all(blocks, "mp", 0, 0, axis_index_groups=groups).reshape(-1, *block.shape[1:])


def both_cores(half):
    return [half, lax.ppermute(half, "mp", SWAP_CORE)]


def own_strip(row_growth, z_hi, mp_index):
    old = row_growth.shape[1]
    strip = old // (NX * NZ)
    mine = pick(row_growth.T.reshape(NX * NZ, strip, -1), mp_index // NC)
    other = lax.ppermute(mine, "dp", SWAP_ZH)
    return jnp.where(z_hi == mp_index % NC, mine, other)


def shards(tokens, cotangent, saved_panels, owners, row_growth, col_growth):
    dp_index, mp_index = lax.axis_index("dp"), lax.axis_index("mp")
    z_hi, y = dp_index // NY, dp_index % NY
    x, core = mp_index // (NZ * NC), mp_index % NC
    place = jnp.stack([y, z_hi, x, core]).astype(jnp.int32)
    slot_of = owners[:, 1] * (MP // SECTIONS) + owners[:, 0]

    slots = panel_slots(saved_panels, y)
    terms = grad_terms(place, tokens, cotangent.T)
    strip = own_strip(row_growth, z_hi, mp_index)
    slots, terms, strip = together(slots, terms, strip)

    rows = panel_rows(slots, slot_of, z_hi, y)
    strips = jnp.concatenate(gather_y(strip))
    rows, terms, strips = together(rows, terms, strips)

    mixed = dot(strips, tokens, NT).astype(BF)
    rows = gather(rows, Z_GROUPS)
    part = sum_y(terms)
    rows, part, mixed = together(rows, part, mixed)

    half = gather(rows, X_GROUPS)
    grads = sum_z(part)
    half, grads, mixed = together(half, grads, mixed)

    grad = pick(grads, z_hi).T
    grads = gather_y(grads.astype(BF))
    source = both_cores(half)
    inners = inner_terms(place, col_growth, source)
    mixed = gather(mixed, Z_GROUPS)
    grads, inners, mixed = together(grads, inners, mixed)

    back = back_block(place, row_growth, grads)
    other = lax.ppermute(back, "dp", SWAP_ZH)
    pair = jnp.where(z_hi == 0, jnp.stack([back, other]), jnp.stack([other, back]))
    mixed = gather(mixed, X_GROUPS).reshape(NX * NZ, NY, -1, mixed.shape[1])
    part, pair = together(sum_y(inners), pair)

    inners = sum_z(part)
    backs = gather_y(pair)
    inners, backs, mixed = together(inners, backs, mixed)

    inners = inners.astype(BF)
    keep, give = row_terms(place, pick(inners, z_hi), grads)
    keep = keep + lax.ppermute(give, "mp", SWAP_CORE).astype(F32)
    keep = lax.all_to_all(keep.astype(BF), "mp", 0, 0, axis_index_groups=PLANE_GROUPS)
    grad_row = keep.astype(F32).sum(axis=0)
    grad_col = col_grad(place, source, backs)
    inners = gather_y(inners)
    mixed, grad_col = together(both_cores(mixed), grad_col)
    grown_out = grown_output(place, mixed, inners).T
    return (grown_out, grad, grad_row, grad_col)


def solution(mesh):
    in_specs = (P("dp", None), P("dp", "mp"), P(None, "mp"), P(), P(None, "dp"), P("mp", "dp"))
    out_specs = (P("dp", "mp"), P("dp", "mp"), P("mp", "dp"), P("mp", "dp"))
    return jax.shard_map(shards, mesh=mesh, in_specs=in_specs, out_specs=out_specs, check_vma=False)
```

```python
import jax
import jax.numpy as jnp
from jax import lax
from jax.experimental import pallas as pl
from jax.experimental.pallas import tpu as pltpu
from jax.sharding import PartitionSpec as P

SECTIONS = 4
ZH, NY = 2, 4
NX, NZ, NC = 4, 4, 2
MP = NX * NZ * NC
PLANE_GROUPS = [[(x * NZ + z) * NC + c for x in range(NX) for z in range(NZ)] for c in range(NC)]
X_GROUPS = [[(x * NZ + z) * NC + c for x in range(NX)] for z in range(NZ) for c in range(NC)]
Z_GROUPS = [[(x * NZ + z) * NC + c for z in range(NZ)] for x in range(NX) for c in range(NC)]
SWAP_ZH = [(i, (i + NY) % (ZH * NY)) for i in range(ZH * NY)]
SWAP_CORE = [(m, m ^ 1) for m in range(MP)]
BF, F32 = jnp.bfloat16, jnp.float32
NN, NT, TN = ((1,), (0,)), ((1,), (1,)), ((0,), (0,))


def shift_y(k):
    return [(h * NY + y, h * NY + (y + k) % NY) for h in range(ZH) for y in range(NY)]


def dot(a, b, dims):
    return lax.dot_general(a, b, (dims, ((), ())), preferred_element_type=F32)


def pick(blocks, index, axis=0):
    return lax.dynamic_index_in_dim(blocks, index, axis, keepdims=False)


def choose(index, cases):
    out = cases[-1]
    for at in range(len(cases) - 1):
        out = jnp.where(index == at, cases[at], out)
    return out


def call(body, place, arrays, outs, flops, scratch=(), limit=40, **specs):
    size = lambda s: s.size * s.dtype.itemsize
    whole = pl.BlockSpec(memory_space=pltpu.VMEM)
    return pl.pallas_call(
        body,
        out_shape=outs,
        grid=specs.get("grid", ()),
        in_specs=[pl.BlockSpec(memory_space=pltpu.SMEM)] + specs.get("in_specs", [whole] * len(arrays)),
        out_specs=specs.get("out_specs", jax.tree.map(lambda _: whole, outs)),
        scratch_shapes=list(scratch),
        compiler_params=pltpu.CompilerParams(vmem_limit_bytes=limit * 2**20),
        cost_estimate=pl.CostEstimate(
            flops=flops,
            bytes_accessed=sum(map(size, arrays)) + sum(map(size, jax.tree.leaves(outs))),
            transcendentals=0,
        ),
    )(place, *arrays)


def struct(shape, kind):
    return jax.ShapeDtypeStruct(shape, kind)


def put(value, k, at, outs):
    for case, out in enumerate(outs):
        @pl.when(k == case)
        def _():
            out[at] = value.astype(out.dtype)


def grad_body(place, tokens, cot, *outs):
    step = pl.program_id(0)
    both = dot(cot[...], tokens[...], NN)
    n = both.shape[1] // 2
    for half in range(2):
        block = 2 * step + half
        put(
            both[:, half * n:(half + 1) * n],
            lax.rem(lax.rem(block, NY) - place[0] + NY, NY),
            block // NY,
            outs,
        )


def grad_terms(place, tokens, cot):
    n = tokens.shape[1] // (ZH * NY)
    hidden = cot.shape[0]
    shape = (ZH, hidden, n)
    outs = [struct(shape, F32)] + [struct(shape, BF)] * (NY - 1)
    full = pl.BlockSpec(shape, lambda s: (0, 0, 0))
    return call(
        grad_body, place, (tokens, cot), outs, 2 * tokens.size * hidden,
        grid=(ZH * NY // 2,),
        in_specs=[
            pl.BlockSpec((tokens.shape[0], 2 * n), lambda s: (0, s)),
            pl.BlockSpec(cot.shape, lambda s: (0, 0)),
        ],
        out_specs=[full] * NY,
    )


def back_body(place, grown, *refs):
    grads, out = refs[:NY], refs[NY]
    n = grads[0].shape[2]
    total = jnp.zeros(out.shape, F32)
    for k in range(NY):
        for h in range(ZH):
            first = (h * NY + lax.rem(place[0] - k + NY, NY)) * n
            total += dot(grads[k][h], grown[pl.ds(pl.multiple_of(first, n), n), :], NN)
    out[...] = total.astype(out.dtype)


def back_block(place, row_growth, grads):
    hidden, old = grads[0].shape[1], row_growth.shape[1]
    return call(
        back_body, place, (row_growth, *grads), struct((hidden, old), BF),
        2 * row_growth.size * hidden,
    )


def inner_body(place, col, mine, other, *outs):
    block = pl.program_id(0)
    k = lax.rem(block - place[0] + NY, NY)
    put(dot(col[...], mine[...], NT), k, place[3], outs)
    put(dot(col[...], other[...], NT), k, 1 - place[3], outs)


def stream(rows, width):
    return pl.BlockSpec((rows, width), lambda s: (s, 0))


def keep_whole(shape):
    return pl.BlockSpec(shape, lambda s: (0,) * len(shape))


def inner_terms(place, col, source):
    hidden, width = col.shape
    rows = source[0].shape[0] // NY
    shape = (ZH, hidden, rows)
    outs = [struct(shape, F32)] + [struct(shape, BF)] * (NY - 1)
    return call(
        inner_body, place, (col, *source), outs, 4 * source[0].size * hidden,
        grid=(NY,),
        in_specs=[keep_whole(col.shape), stream(rows, width), stream(rows, width)],
        out_specs=[keep_whole(shape)] * NY,
    )


def col_body(place, mine, other, *refs):
    back, out, held = refs[:NY], refs[NY], refs[NY + 1]
    block = pl.program_id(0)

    @pl.when(block == 0)
    def _():
        for k in range(NY):
            held[k] = back[k][...]
        out[...] = jnp.zeros(out.shape, F32)

    k = lax.rem(place[0] - block + NY, NY)
    out[...] += dot(held[k, place[3]], mine[...], NN) + dot(held[k, 1 - place[3]], other[...], NN)


def col_grad(place, source, back):
    hidden, rows = back[0].shape[1:]
    width = source[0].shape[1]
    return call(
        col_body, place, (*source, *back), struct((hidden, width), F32),
        4 * source[0].size * hidden,
        scratch=[pltpu.VMEM((NY, *back[0].shape), BF)],
        limit=56,
        grid=(NY,),
        in_specs=[stream(rows, width)] * 2 + [keep_whole(back[0].shape)] * NY,
        out_specs=keep_whole((hidden, width)),
    )


def row_body(place, inner, *refs):
    grads, keep, give = refs[:NY], refs[NY], refs[NY + 1]
    rows = keep.shape[1]
    for k in range(NY):
        for h in range(ZH):
            block = dot(grads[k][h], inner[...], TN)
            at = (h * NY + lax.rem(place[0] - k + NY, NY)) * 2
            for q in range(2):
                one = block[2 * q * rows:(2 * q + 1) * rows]
                two = block[(2 * q + 1) * rows:(2 * q + 2) * rows]
                first = place[3] == 0
                keep[at + q] = jnp.where(first, one, two)
                give[at + q] = jnp.where(first, two, one).astype(BF)


def row_terms(place, inner, grads):
    old, n = inner.shape[1], grads[0].shape[2]
    shape = (NX * NZ, n * ZH * NY // MP, old)
    return call(
        row_body, place, (inner, *grads), [struct(shape, F32), struct(shape, BF)],
        2 * inner.size * n * ZH * NY,
    )


def out_body(place, mixed, *refs):
    inner, out = refs[:NY], refs[NY]
    total = jnp.zeros(out.shape, F32)
    for k in range(NY):
        for h in range(ZH):
            rows = mixed[:, h, k]
            total += dot(inner[k][h], rows.reshape(-1, out.shape[1]), NN)
    out[...] = total.astype(out.dtype)


def grown_output(place, mixed, inner):
    hidden, count = inner[0].shape[1], mixed.shape[-1]
    part = count // 4
    return call(
        out_body, place, (mixed, *inner), struct((hidden, count), BF),
        2 * mixed.size * hidden,
        limit=56,
        grid=(count // part,),
        in_specs=[pl.BlockSpec((*mixed.shape[:-1], part), lambda s: (0, 0, 0, 0, s))]
        + [keep_whole(inner[0].shape)] * NY,
        out_specs=pl.BlockSpec((hidden, part), lambda s: (0, s)),
    )


def together(*values):
    return lax.optimization_barrier(values)


def exchange_y(block_for):
    got = {k: lax.ppermute(block_for(k), "dp", shift_y(k)) for k in (2, 1, 3)}
    return [None, got[1], got[2], got[3]]


def sum_y(blocks):
    got = exchange_y(lambda k: blocks[k])
    return blocks[0] + got[1].astype(F32) + got[2].astype(F32) + got[3].astype(F32)


def sum_z(part):
    return part + lax.ppermute(part.astype(BF), "dp", SWAP_ZH).astype(F32)


def gather_y(block):
    return [block] + exchange_y(lambda k: block)[1:]


def panel_slots(saved, y):
    width = saved.shape[1]
    sub = saved.shape[0] // (MP * NY)
    rows = saved.reshape(NC, NX, NZ, NY, sub, width)
    mine = pick(rows, y, 3).transpose(1, 2, 0, 3, 4).reshape(MP, sub, width)
    return lax.all_to_all(mine, "mp", 0, 0)


def panel_rows(slots, slot_of, z_hi, y):
    sub, width = slots.shape[1:]
    panels = jnp.take(slots, slot_of, axis=0).reshape(ZH, NY, -1, sub, width)
    panels = pick(panels, z_hi)
    got = exchange_y(lambda k: pick(panels, (y + k) % NY))
    got[0] = pick(panels, y)
    chunk = jnp.stack([choose((y - j) % NY, got) for j in range(NY)])
    return chunk.transpose(0, 2, 1, 3).reshape(NY * sub, -1)


def gather(block, groups):
    blocks = jnp.broadcast_to(block[None], (len(groups[0]), *block.shape))
    return lax.all_to_all(blocks, "mp", 0, 0, axis_index_groups=groups).reshape(-1, *block.shape[1:])


def both_cores(half):
    return [half, lax.ppermute(half, "mp", SWAP_CORE)]


def own_strip(row_growth, z_hi, mp_index):
    old = row_growth.shape[1]
    strip = old // (NX * NZ)
    mine = pick(row_growth.T.reshape(NX * NZ, strip, -1), mp_index // NC)
    other = lax.ppermute(mine, "dp", SWAP_ZH)
    return jnp.where(z_hi == mp_index % NC, mine, other)


def shards(tokens, cotangent, saved_panels, owners, row_growth, col_growth):
    dp_index, mp_index = lax.axis_index("dp"), lax.axis_index("mp")
    z_hi, y = dp_index // NY, dp_index % NY
    x, core = mp_index // (NZ * NC), mp_index % NC
    place = jnp.stack([y, z_hi, x, core]).astype(jnp.int32)
    slot_of = owners[:, 1] * (MP // SECTIONS) + owners[:, 0]

    slots = panel_slots(saved_panels, y)
    part = sum_y(grad_terms(place, tokens, cotangent.T))
    slots, part = together(slots, part)

    grads = sum_z(part)
    strip = own_strip(row_growth, z_hi, mp_index)
    rows = gather(panel_rows(slots, slot_of, z_hi, y), Z_GROUPS)
    rows, grads, strip = together(rows, grads, strip)

    grad = pick(grads, z_hi).T
    grads = gather_y(grads.astype(BF))
    strips = jnp.concatenate(gather_y(strip))
    mixed = dot(strips, tokens, NT).astype(BF)
    half = gather(rows, X_GROUPS)
    half, grads, mixed = together(half, grads, mixed)

    mixed = lax.all_gather(mixed, "mp", axis=0, tiled=True)
    mixed = mixed.reshape(NX * NZ, NC, NY, -1, tokens.shape[0])
    back = back_block(place, row_growth, grads)
    other = lax.ppermute(back, "dp", SWAP_ZH)
    pair = jnp.where(z_hi == 0, jnp.stack([back, other]), jnp.stack([other, back]))
    source = both_cores(half)
    inners = inner_terms(place, col_growth, source)
    inners, pair = together(inners, pair)

    part, pair = together(sum_y(inners), pair)

    inners = sum_z(part)
    backs = gather_y(pair)
    inners, backs = together(inners, backs)

    inners = inners.astype(BF)
    keep, give = row_terms(place, pick(inners, z_hi), grads)
    keep = keep + lax.ppermute(give, "mp", SWAP_CORE).astype(F32)
    keep = lax.all_to_all(keep.astype(BF), "mp", 0, 0, axis_index_groups=PLANE_GROUPS)
    grad_row = keep.astype(F32).sum(axis=0)
    grad_col = col_grad(place, source, backs)
    inners = gather_y(inners)
    mixed, grad_col = together(mixed, grad_col)
    grown_out = grown_output(place, mixed, inners).T
    return (grown_out, grad, grad_row, grad_col)


def solution(mesh):
    in_specs = (P("dp", None), P("dp", "mp"), P(None, "mp"), P(), P(None, "dp"), P("mp", "dp"))
    out_specs = (P("dp", "mp"), P("dp", "mp"), P("mp", "dp"), P("mp", "dp"))
    return jax.shard_map(shards, mesh=mesh, in_specs=in_specs, out_specs=out_specs, check_vma=False)
```

```python
import jax
import jax.numpy as jnp
from jax import lax
from jax.experimental import pallas as pl
from jax.experimental.pallas import tpu as pltpu
from jax.sharding import PartitionSpec as P

SECTIONS = 4
ZH, NY = 2, 4
NX, NZ, NC = 4, 4, 2
MP = NX * NZ * NC
PLANE_GROUPS = [[(x * NZ + z) * NC + c for x in range(NX) for z in range(NZ)] for c in range(NC)]
X_GROUPS = [[(x * NZ + z) * NC + c for x in range(NX)] for z in range(NZ) for c in range(NC)]
Z_GROUPS = [[(x * NZ + z) * NC + c for z in range(NZ)] for x in range(NX) for c in range(NC)]
SWAP_ZH = [(i, (i + NY) % (ZH * NY)) for i in range(ZH * NY)]
SWAP_CORE = [(m, m ^ 1) for m in range(MP)]
BF, F32 = jnp.bfloat16, jnp.float32
NN, NT, TN = ((1,), (0,)), ((1,), (1,)), ((0,), (0,))


def shift_y(k):
    return [(h * NY + y, h * NY + (y + k) % NY) for h in range(ZH) for y in range(NY)]


def dot(a, b, dims):
    return lax.dot_general(a, b, (dims, ((), ())), preferred_element_type=F32)


def pick(blocks, index, axis=0):
    return lax.dynamic_index_in_dim(blocks, index, axis, keepdims=False)


def choose(index, cases):
    out = cases[-1]
    for at in range(len(cases) - 1):
        out = jnp.where(index == at, cases[at], out)
    return out


def call(body, place, arrays, outs, flops, scratch=(), limit=40, **specs):
    size = lambda s: s.size * s.dtype.itemsize
    whole = pl.BlockSpec(memory_space=pltpu.VMEM)
    return pl.pallas_call(
        body,
        out_shape=outs,
        grid=specs.get("grid", ()),
        in_specs=[pl.BlockSpec(memory_space=pltpu.SMEM)] + specs.get("in_specs", [whole] * len(arrays)),
        out_specs=specs.get("out_specs", jax.tree.map(lambda _: whole, outs)),
        scratch_shapes=list(scratch),
        compiler_params=pltpu.CompilerParams(vmem_limit_bytes=limit * 2**20),
        cost_estimate=pl.CostEstimate(
            flops=flops,
            bytes_accessed=sum(map(size, arrays)) + sum(map(size, jax.tree.leaves(outs))),
            transcendentals=0,
        ),
    )(place, *arrays)


def struct(shape, kind):
    return jax.ShapeDtypeStruct(shape, kind)


def put(value, k, at, outs):
    for case, out in enumerate(outs):
        @pl.when(k == case)
        def _():
            out[at] = value.astype(out.dtype)


def grad_body(place, tokens, cot, *outs):
    step = pl.program_id(0)
    both = dot(cot[...], tokens[...], NN)
    n = both.shape[1] // 2
    for half in range(2):
        block = 2 * step + half
        put(
            both[:, half * n:(half + 1) * n],
            lax.rem(lax.rem(block, NY) - place[0] + NY, NY),
            block // NY,
            outs,
        )


def grad_terms(place, tokens, cot):
    n = tokens.shape[1] // (ZH * NY)
    hidden = cot.shape[0]
    shape = (ZH, hidden, n)
    outs = [struct(shape, F32)] + [struct(shape, BF)] * (NY - 1)
    full = pl.BlockSpec(shape, lambda s: (0, 0, 0))
    return call(
        grad_body, place, (tokens, cot), outs, 2 * tokens.size * hidden,
        grid=(ZH * NY // 2,),
        in_specs=[
            pl.BlockSpec((tokens.shape[0], 2 * n), lambda s: (0, s)),
            pl.BlockSpec(cot.shape, lambda s: (0, 0)),
        ],
        out_specs=[full] * NY,
    )


def back_body(place, grown, *refs):
    grads, out = refs[:NY], refs[NY]
    n = grads[0].shape[2]
    total = jnp.zeros(out.shape, F32)
    for k in range(NY):
        for h in range(ZH):
            first = (h * NY + lax.rem(place[0] - k + NY, NY)) * n
            total += dot(grads[k][h], grown[pl.ds(pl.multiple_of(first, n), n), :], NN)
    out[...] = total.astype(out.dtype)


def back_block(place, row_growth, grads):
    hidden, old = grads[0].shape[1], row_growth.shape[1]
    return call(
        back_body, place, (row_growth, *grads), struct((hidden, old), BF),
        2 * row_growth.size * hidden,
    )


def inner_body(place, col, mine, other, *outs):
    block = pl.program_id(0)
    k = lax.rem(block - place[0] + NY, NY)
    put(dot(col[...], mine[...], NT), k, place[3], outs)
    put(dot(col[...], other[...], NT), k, 1 - place[3], outs)


def stream(rows, width):
    return pl.BlockSpec((rows, width), lambda s: (s, 0))


def keep_whole(shape):
    return pl.BlockSpec(shape, lambda s: (0,) * len(shape))


def inner_terms(place, col, source):
    hidden, width = col.shape
    rows = source[0].shape[0] // NY
    shape = (ZH, hidden, rows)
    outs = [struct(shape, F32)] + [struct(shape, BF)] * (NY - 1)
    return call(
        inner_body, place, (col, *source), outs, 4 * source[0].size * hidden,
        grid=(NY,),
        in_specs=[keep_whole(col.shape), stream(rows, width), stream(rows, width)],
        out_specs=[keep_whole(shape)] * NY,
    )


def col_body(place, mine, other, *refs):
    back, out, held = refs[:NY], refs[NY], refs[NY + 1]
    block = pl.program_id(0)

    @pl.when(block == 0)
    def _():
        for k in range(NY):
            held[k] = back[k][...]
        out[...] = jnp.zeros(out.shape, F32)

    k = lax.rem(place[0] - block + NY, NY)
    out[...] += dot(held[k, place[3]], mine[...], NN) + dot(held[k, 1 - place[3]], other[...], NN)


def col_grad(place, source, back):
    hidden, rows = back[0].shape[1:]
    width = source[0].shape[1]
    return call(
        col_body, place, (*source, *back), struct((hidden, width), F32),
        4 * source[0].size * hidden,
        scratch=[pltpu.VMEM((NY, *back[0].shape), BF)],
        limit=56,
        grid=(NY,),
        in_specs=[stream(rows, width)] * 2 + [keep_whole(back[0].shape)] * NY,
        out_specs=keep_whole((hidden, width)),
    )


def row_body(place, inner, *refs):
    grads, keep, give = refs[:NY], refs[NY], refs[NY + 1]
    rows = keep.shape[1]
    for k in range(NY):
        for h in range(ZH):
            block = dot(grads[k][h], inner[...], TN)
            at = (h * NY + lax.rem(place[0] - k + NY, NY)) * 2
            for q in range(2):
                one = block[2 * q * rows:(2 * q + 1) * rows]
                two = block[(2 * q + 1) * rows:(2 * q + 2) * rows]
                first = place[3] == 0
                keep[at + q] = jnp.where(first, one, two)
                give[at + q] = jnp.where(first, two, one).astype(BF)


def row_terms(place, inner, grads):
    old, n = inner.shape[1], grads[0].shape[2]
    shape = (NX * NZ, n * ZH * NY // MP, old)
    return call(
        row_body, place, (inner, *grads), [struct(shape, F32), struct(shape, BF)],
        2 * inner.size * n * ZH * NY,
    )


def out_body(place, mixed, *refs):
    inner, out = refs[:NY], refs[NY]
    total = jnp.zeros(out.shape, F32)
    for k in range(NY):
        for h in range(ZH):
            rows = mixed[:, h, k]
            total += dot(inner[k][h], rows.reshape(-1, out.shape[1]), NN)
    out[...] = total.astype(out.dtype)


def grown_output(place, mixed, inner):
    hidden, count = inner[0].shape[1], mixed.shape[-1]
    part = count // 4
    return call(
        out_body, place, (mixed, *inner), struct((hidden, count), BF),
        2 * mixed.size * hidden,
        limit=56,
        grid=(count // part,),
        in_specs=[pl.BlockSpec((*mixed.shape[:-1], part), lambda s: (0, 0, 0, 0, s))]
        + [keep_whole(inner[0].shape)] * NY,
        out_specs=pl.BlockSpec((hidden, part), lambda s: (0, s)),
    )


def together(*values):
    return lax.optimization_barrier(values)


def exchange_y(block_for):
    got = {k: lax.ppermute(block_for(k), "dp", shift_y(k)) for k in (2, 1, 3)}
    return [None, got[1], got[2], got[3]]


def sum_y(blocks):
    got = exchange_y(lambda k: blocks[k])
    return blocks[0] + got[1].astype(F32) + got[2].astype(F32) + got[3].astype(F32)


def sum_z(part):
    return part + lax.ppermute(part.astype(BF), "dp", SWAP_ZH).astype(F32)


def gather_y(block):
    return [block] + exchange_y(lambda k: block)[1:]


def panel_slots(saved, y):
    width = saved.shape[1]
    sub = saved.shape[0] // (MP * NY)
    rows = saved.reshape(NC, NX, NZ, NY, sub, width)
    mine = pick(rows, y, 3).transpose(1, 2, 0, 3, 4).reshape(MP, sub, width)
    return lax.all_to_all(mine, "mp", 0, 0)


def panel_rows(slots, slot_of, z_hi, y):
    sub, width = slots.shape[1:]
    panels = jnp.take(slots, slot_of, axis=0).reshape(ZH, NY, -1, sub, width)
    panels = pick(panels, z_hi)
    got = exchange_y(lambda k: pick(panels, (y + k) % NY))
    got[0] = pick(panels, y)
    chunk = jnp.stack([choose((y - j) % NY, got) for j in range(NY)])
    return chunk.transpose(0, 2, 1, 3).reshape(NY * sub, -1)


def gather(block, groups):
    blocks = jnp.broadcast_to(block[None], (len(groups[0]), *block.shape))
    return lax.all_to_all(blocks, "mp", 0, 0, axis_index_groups=groups).reshape(-1, *block.shape[1:])


def both_cores(half):
    return [half, lax.ppermute(half, "mp", SWAP_CORE)]


def own_strip(row_growth, z_hi, mp_index):
    old = row_growth.shape[1]
    strip = old // (NX * NZ)
    mine = pick(row_growth.T.reshape(NX * NZ, strip, -1), mp_index // NC)
    other = lax.ppermute(mine, "dp", SWAP_ZH)
    return jnp.where(z_hi == mp_index % NC, mine, other)


def shards(tokens, cotangent, saved_panels, owners, row_growth, col_growth):
    dp_index, mp_index = lax.axis_index("dp"), lax.axis_index("mp")
    z_hi, y = dp_index // NY, dp_index % NY
    x, core = mp_index // (NZ * NC), mp_index % NC
    place = jnp.stack([y, z_hi, x, core]).astype(jnp.int32)
    slot_of = owners[:, 1] * (MP // SECTIONS) + owners[:, 0]

    slots = panel_slots(saved_panels, y)
    part = sum_y(grad_terms(place, tokens, cotangent.T))
    slots, part = together(slots, part)

    grads = sum_z(part)
    rows = panel_rows(slots, slot_of, z_hi, y)
    rows, grads = together(rows, grads)

    grad = pick(grads, z_hi).T
    grads = gather_y(grads.astype(BF))
    strip = own_strip(row_growth, z_hi, mp_index)
    rows = gather(rows, Z_GROUPS)
    rows, grads, strip = together(rows, grads, strip)

    back = back_block(place, row_growth, grads)
    other = lax.ppermute(back, "dp", SWAP_ZH)
    pair = jnp.where(z_hi == 0, jnp.stack([back, other]), jnp.stack([other, back]))
    strips = jnp.concatenate(gather_y(strip))
    mixed = dot(strips, tokens, NT).astype(BF)
    half = gather(rows, X_GROUPS)
    half, pair, mixed = together(half, pair, mixed)

    mixed = lax.all_gather(mixed, "mp", axis=0, tiled=True)
    mixed = mixed.reshape(NX * NZ, NC, NY, -1, tokens.shape[0])
    source = both_cores(half)
    inners = inner_terms(place, col_growth, source)
    part, pair = together(sum_y(inners), pair)

    inners = sum_z(part)
    backs = gather_y(pair)
    inners, backs = together(inners, backs)

    inners = inners.astype(BF)
    keep, give = row_terms(place, pick(inners, z_hi), grads)
    keep = keep + lax.ppermute(give, "mp", SWAP_CORE).astype(F32)
    keep = lax.all_to_all(keep.astype(BF), "mp", 0, 0, axis_index_groups=PLANE_GROUPS)
    grad_row = keep.astype(F32).sum(axis=0)
    grad_col = col_grad(place, source, backs)
    inners = gather_y(inners)
    mixed, grad_col = together(mixed, grad_col)
    grown_out = grown_output(place, mixed, inners).T
    return (grown_out, grad, grad_row, grad_col)


def solution(mesh):
    in_specs = (P("dp", None), P("dp", "mp"), P(None, "mp"), P(), P(None, "dp"), P("mp", "dp"))
    out_specs = (P("dp", "mp"), P("dp", "mp"), P("mp", "dp"), P("mp", "dp"))
    return jax.shard_map(shards, mesh=mesh, in_specs=in_specs, out_specs=out_specs, check_vma=False)
```

```python
import jax
import jax.numpy as jnp
from jax import lax
from jax.experimental import pallas as pl
from jax.experimental.pallas import tpu as pltpu
from jax.sharding import PartitionSpec as P

SECTIONS = 4
ZH, NY = 2, 4
NX, NZ, NC = 4, 4, 2
MP = NX * NZ * NC
PLANE_GROUPS = [[(x * NZ + z) * NC + c for x in range(NX) for z in range(NZ)] for c in range(NC)]
X_GROUPS = [[(x * NZ + z) * NC + c for x in range(NX)] for z in range(NZ) for c in range(NC)]
Z_GROUPS = [[(x * NZ + z) * NC + c for z in range(NZ)] for x in range(NX) for c in range(NC)]
SWAP_ZH = [(i, (i + NY) % (ZH * NY)) for i in range(ZH * NY)]
SWAP_CORE = [(m, m ^ 1) for m in range(MP)]
BF, F32 = jnp.bfloat16, jnp.float32
NN, NT, TN = ((1,), (0,)), ((1,), (1,)), ((0,), (0,))


def shift_y(k):
    return [(h * NY + y, h * NY + (y + k) % NY) for h in range(ZH) for y in range(NY)]


def dot(a, b, dims):
    return lax.dot_general(a, b, (dims, ((), ())), preferred_element_type=F32)


def pick(blocks, index, axis=0):
    return lax.dynamic_index_in_dim(blocks, index, axis, keepdims=False)


def choose(index, cases):
    out = cases[-1]
    for at in range(len(cases) - 1):
        out = jnp.where(index == at, cases[at], out)
    return out


def call(body, place, arrays, outs, flops, scratch=(), limit=40, **specs):
    size = lambda s: s.size * s.dtype.itemsize
    whole = pl.BlockSpec(memory_space=pltpu.VMEM)
    return pl.pallas_call(
        body,
        out_shape=outs,
        grid=specs.get("grid", ()),
        in_specs=[pl.BlockSpec(memory_space=pltpu.SMEM)] + specs.get("in_specs", [whole] * len(arrays)),
        out_specs=specs.get("out_specs", jax.tree.map(lambda _: whole, outs)),
        scratch_shapes=list(scratch),
        compiler_params=pltpu.CompilerParams(vmem_limit_bytes=limit * 2**20),
        cost_estimate=pl.CostEstimate(
            flops=flops,
            bytes_accessed=sum(map(size, arrays)) + sum(map(size, jax.tree.leaves(outs))),
            transcendentals=0,
        ),
    )(place, *arrays)


def struct(shape, kind):
    return jax.ShapeDtypeStruct(shape, kind)


def put(value, k, at, outs):
    for case, out in enumerate(outs):
        @pl.when(k == case)
        def _():
            out[at] = value.astype(out.dtype)


def grad_body(place, tokens, cot, *outs):
    step = pl.program_id(0)
    both = dot(cot[...], tokens[...], NN)
    n = both.shape[1] // 2
    for half in range(2):
        block = 2 * step + half
        put(
            both[:, half * n:(half + 1) * n],
            lax.rem(lax.rem(block, NY) - place[0] + NY, NY),
            block // NY,
            outs,
        )


def grad_terms(place, tokens, cot):
    n = tokens.shape[1] // (ZH * NY)
    hidden = cot.shape[0]
    shape = (ZH, hidden, n)
    outs = [struct(shape, F32)] + [struct(shape, BF)] * (NY - 1)
    full = pl.BlockSpec(shape, lambda s: (0, 0, 0))
    return call(
        grad_body, place, (tokens, cot), outs, 2 * tokens.size * hidden,
        limit=56,
        grid=(ZH * NY // 2,),
        in_specs=[
            pl.BlockSpec((tokens.shape[0], 2 * n), lambda s: (0, s)),
            pl.BlockSpec(cot.shape, lambda s: (0, 0)),
        ],
        out_specs=[full] * NY,
    )


def back_body(place, grown, *refs):
    grads, out = refs[:NY], refs[NY]
    n = grads[0].shape[2]
    total = jnp.zeros(out.shape, F32)
    for k in range(NY):
        for h in range(ZH):
            first = (h * NY + lax.rem(place[0] - k + NY, NY)) * n
            total += dot(grads[k][h], grown[pl.ds(pl.multiple_of(first, n), n), :], NN)
    out[...] = total.astype(out.dtype)


def back_block(place, row_growth, grads):
    hidden, old = grads[0].shape[1], row_growth.shape[1]
    return call(
        back_body, place, (row_growth, *grads), struct((hidden, old), BF),
        2 * row_growth.size * hidden, limit=56,
    )


def inner_body(place, col, mine, other, *outs):
    block = pl.program_id(0)
    k = lax.rem(block - place[0] + NY, NY)
    put(dot(col[...], mine[...], NT), k, place[3], outs)
    put(dot(col[...], other[...], NT), k, 1 - place[3], outs)


def stream(rows, width):
    return pl.BlockSpec((rows, width), lambda s: (s, 0))


def keep_whole(shape):
    return pl.BlockSpec(shape, lambda s: (0,) * len(shape))


def inner_terms(place, col, source):
    hidden, width = col.shape
    rows = source[0].shape[0] // NY
    shape = (ZH, hidden, rows)
    outs = [struct(shape, F32)] + [struct(shape, BF)] * (NY - 1)
    return call(
        inner_body, place, (col, *source), outs, 4 * source[0].size * hidden,
        grid=(NY,),
        in_specs=[keep_whole(col.shape), stream(rows, width), stream(rows, width)],
        out_specs=[keep_whole(shape)] * NY,
    )


def col_body(place, mine, other, *refs):
    back, out, held = refs[:NY], refs[NY], refs[NY + 1]
    block = pl.program_id(0)

    @pl.when(block == 0)
    def _():
        for k in range(NY):
            held[k] = back[k][...]
        out[...] = jnp.zeros(out.shape, F32)

    k = lax.rem(place[0] - block + NY, NY)
    out[...] += dot(held[k, place[3]], mine[...], NN) + dot(held[k, 1 - place[3]], other[...], NN)


def col_grad(place, source, back):
    hidden, rows = back[0].shape[1:]
    width = source[0].shape[1]
    return call(
        col_body, place, (*source, *back), struct((hidden, width), F32),
        4 * source[0].size * hidden,
        scratch=[pltpu.VMEM((NY, *back[0].shape), BF)],
        limit=56,
        grid=(NY,),
        in_specs=[stream(rows, width)] * 2 + [keep_whole(back[0].shape)] * NY,
        out_specs=keep_whole((hidden, width)),
    )


def row_body(place, inner, *refs):
    grads, keep, give = refs[:NY], refs[NY], refs[NY + 1]
    rows = keep.shape[1]
    for k in range(NY):
        for h in range(ZH):
            block = dot(grads[k][h], inner[...], TN)
            at = (h * NY + lax.rem(place[0] - k + NY, NY)) * 2
            for q in range(2):
                one = block[2 * q * rows:(2 * q + 1) * rows]
                two = block[(2 * q + 1) * rows:(2 * q + 2) * rows]
                first = place[3] == 0
                keep[at + q] = jnp.where(first, one, two)
                give[at + q] = jnp.where(first, two, one).astype(BF)


def row_terms(place, inner, grads):
    old, n = inner.shape[1], grads[0].shape[2]
    shape = (NX * NZ, n * ZH * NY // MP, old)
    return call(
        row_body, place, (inner, *grads), [struct(shape, F32), struct(shape, BF)],
        2 * inner.size * n * ZH * NY, limit=56,
    )


def out_body(place, mixed, *refs):
    inner, out = refs[:NY], refs[NY]
    total = jnp.zeros(out.shape, F32)
    for k in range(NY):
        for h in range(ZH):
            rows = mixed[:, h, k]
            total += dot(inner[k][h], rows.reshape(-1, out.shape[1]), NN)
    out[...] = total.astype(out.dtype)


def grown_output(place, mixed, inner):
    hidden, count = inner[0].shape[1], mixed.shape[-1]
    part = count // 4
    return call(
        out_body, place, (mixed, *inner), struct((hidden, count), BF),
        2 * mixed.size * hidden,
        limit=56,
        grid=(count // part,),
        in_specs=[pl.BlockSpec((*mixed.shape[:-1], part), lambda s: (0, 0, 0, 0, s))]
        + [keep_whole(inner[0].shape)] * NY,
        out_specs=pl.BlockSpec((hidden, part), lambda s: (0, s)),
    )


def together(*values):
    return lax.optimization_barrier(values)


def exchange_y(block_for):
    got = {k: lax.ppermute(block_for(k), "dp", shift_y(k)) for k in (2, 1, 3)}
    return [None, got[1], got[2], got[3]]


def sum_y(blocks):
    got = exchange_y(lambda k: blocks[k])
    return blocks[0] + got[1].astype(F32) + got[2].astype(F32) + got[3].astype(F32)


def sum_z(part):
    return part + lax.ppermute(part.astype(BF), "dp", SWAP_ZH).astype(F32)


def gather_y(block):
    return [block] + exchange_y(lambda k: block)[1:]


def panel_slots(saved, y):
    width = saved.shape[1]
    sub = saved.shape[0] // (MP * NY)
    rows = saved.reshape(NC, NX, NZ, NY, sub, width)
    mine = pick(rows, y, 3).transpose(1, 2, 0, 3, 4).reshape(MP, sub, width)
    return lax.all_to_all(mine, "mp", 0, 0)


def panel_rows(slots, slot_of, z_hi, y):
    sub, width = slots.shape[1:]
    panels = jnp.take(slots, slot_of, axis=0).reshape(ZH, NY, -1, sub, width)
    panels = pick(panels, z_hi)
    got = exchange_y(lambda k: pick(panels, (y + k) % NY))
    got[0] = pick(panels, y)
    chunk = jnp.stack([choose((y - j) % NY, got) for j in range(NY)])
    return chunk.transpose(0, 2, 1, 3).reshape(NY * sub, -1)


def gather(block, groups):
    blocks = jnp.broadcast_to(block[None], (len(groups[0]), *block.shape))
    return lax.all_to_all(blocks, "mp", 0, 0, axis_index_groups=groups).reshape(-1, *block.shape[1:])


def both_cores(half):
    return [half, lax.ppermute(half, "mp", SWAP_CORE)]


def own_strip(row_growth, z_hi, mp_index):
    old = row_growth.shape[1]
    strip = old // (NX * NZ)
    mine = pick(row_growth.T.reshape(NX * NZ, strip, -1), mp_index // NC)
    other = lax.ppermute(mine, "dp", SWAP_ZH)
    return jnp.where(z_hi == mp_index % NC, mine, other)


def shards(tokens, cotangent, saved_panels, owners, row_growth, col_growth):
    dp_index, mp_index = lax.axis_index("dp"), lax.axis_index("mp")
    z_hi, y = dp_index // NY, dp_index % NY
    x, core = mp_index // (NZ * NC), mp_index % NC
    place = jnp.stack([y, z_hi, x, core]).astype(jnp.int32)
    slot_of = owners[:, 1] * (MP // SECTIONS) + owners[:, 0]

    slots = panel_slots(saved_panels, y)
    part = sum_y(grad_terms(place, tokens, cotangent.T))
    slots, part = together(slots, part)

    grads = sum_z(part)
    rows = panel_rows(slots, slot_of, z_hi, y)
    rows, grads = together(rows, grads)

    strip = own_strip(row_growth, z_hi, mp_index)
    rows = gather(rows, Z_GROUPS)
    rows, grads, strip = together(rows, grads, strip)

    grad = pick(grads, z_hi).T
    grads = gather_y(grads.astype(BF))
    strips = jnp.concatenate(gather_y(strip))
    mixed = dot(strips, tokens, NT).astype(BF)
    half = gather(rows, X_GROUPS)
    half, grads, mixed = together(half, grads, mixed)

    mixed = lax.all_gather(mixed, "mp", axis=0, tiled=True)
    mixed = mixed.reshape(NX * NZ, NC, NY, -1, tokens.shape[0])
    source = both_cores(half)
    inners = inner_terms(place, col_growth, source)
    back = back_block(place, row_growth, grads)
    other = lax.ppermute(back, "dp", SWAP_ZH)
    pair = jnp.where(z_hi == 0, jnp.stack([back, other]), jnp.stack([other, back]))
    part, pair = together(sum_y(inners), pair)

    inners = sum_z(part)
    backs = gather_y(pair)
    inners, backs = together(inners, backs)

    inners = inners.astype(BF)
    keep, give = row_terms(place, pick(inners, z_hi), grads)
    keep = keep + lax.ppermute(give, "mp", SWAP_CORE).astype(F32)
    keep = lax.all_to_all(keep.astype(BF), "mp", 0, 0, axis_index_groups=PLANE_GROUPS)
    grad_row = keep.astype(F32).sum(axis=0)
    grad_col = col_grad(place, source, backs)
    inners = gather_y(inners)
    mixed, grad_col = together(mixed, grad_col)
    grown_out = grown_output(place, mixed, inners).T
    return (grown_out, grad, grad_row, grad_col)


def solution(mesh):
    in_specs = (P("dp", None), P("dp", "mp"), P(None, "mp"), P(), P(None, "dp"), P("mp", "dp"))
    out_specs = (P("dp", "mp"), P("dp", "mp"), P("mp", "dp"), P("mp", "dp"))
    return jax.shard_map(shards, mesh=mesh, in_specs=in_specs, out_specs=out_specs, check_vma=False)
```

```python
import jax
import jax.numpy as jnp
from jax import lax
from jax.experimental import pallas as pl
from jax.experimental.pallas import tpu as pltpu
from jax.sharding import PartitionSpec as P

SECTIONS = 4
ZH, NY = 2, 4
NX, NZ, NC = 4, 4, 2
MP = NX * NZ * NC
PLANE_GROUPS = [[(x * NZ + z) * NC + c for x in range(NX) for z in range(NZ)] for c in range(NC)]
X_GROUPS = [[(x * NZ + z) * NC + c for x in range(NX)] for z in range(NZ) for c in range(NC)]
Z_GROUPS = [[(x * NZ + z) * NC + c for z in range(NZ)] for x in range(NX) for c in range(NC)]
SWAP_ZH = [(i, (i + NY) % (ZH * NY)) for i in range(ZH * NY)]
SWAP_CORE = [(m, m ^ 1) for m in range(MP)]
BF, F32 = jnp.bfloat16, jnp.float32
NN, NT, TN = ((1,), (0,)), ((1,), (1,)), ((0,), (0,))


def shift_y(k):
    return [(h * NY + y, h * NY + (y + k) % NY) for h in range(ZH) for y in range(NY)]


def dot(a, b, dims):
    return lax.dot_general(a, b, (dims, ((), ())), preferred_element_type=F32)


def pick(blocks, index, axis=0):
    return lax.dynamic_index_in_dim(blocks, index, axis, keepdims=False)


def choose(index, cases):
    out = cases[-1]
    for at in range(len(cases) - 1):
        out = jnp.where(index == at, cases[at], out)
    return out


def call(body, place, arrays, outs, flops, scratch=(), limit=40, **specs):
    size = lambda s: s.size * s.dtype.itemsize
    whole = pl.BlockSpec(memory_space=pltpu.VMEM)
    return pl.pallas_call(
        body,
        out_shape=outs,
        grid=specs.get("grid", ()),
        in_specs=[pl.BlockSpec(memory_space=pltpu.SMEM)] + specs.get("in_specs", [whole] * len(arrays)),
        out_specs=specs.get("out_specs", jax.tree.map(lambda _: whole, outs)),
        scratch_shapes=list(scratch),
        compiler_params=pltpu.CompilerParams(vmem_limit_bytes=limit * 2**20),
        cost_estimate=pl.CostEstimate(
            flops=flops,
            bytes_accessed=sum(map(size, arrays)) + sum(map(size, jax.tree.leaves(outs))),
            transcendentals=0,
        ),
    )(place, *arrays)


def struct(shape, kind):
    return jax.ShapeDtypeStruct(shape, kind)


def put(value, k, at, outs):
    for case, out in enumerate(outs):
        @pl.when(k == case)
        def _():
            out[at] = value.astype(out.dtype)


def grad_body(place, tokens, cot, *outs):
    step = pl.program_id(0)
    both = dot(cot[...], tokens[...], NN)
    n = both.shape[1] // 2
    for half in range(2):
        block = 2 * step + half
        put(
            both[:, half * n:(half + 1) * n],
            lax.rem(lax.rem(block, NY) - place[0] + NY, NY),
            block // NY,
            outs,
        )


def grad_terms(place, tokens, cot):
    n = tokens.shape[1] // (ZH * NY)
    hidden = cot.shape[0]
    shape = (ZH, hidden, n)
    outs = [struct(shape, F32)] + [struct(shape, BF)] * (NY - 1)
    full = pl.BlockSpec(shape, lambda s: (0, 0, 0))
    return call(
        grad_body, place, (tokens, cot), outs, 2 * tokens.size * hidden,
        limit=56,
        grid=(ZH * NY // 2,),
        in_specs=[
            pl.BlockSpec((tokens.shape[0], 2 * n), lambda s: (0, s)),
            pl.BlockSpec(cot.shape, lambda s: (0, 0)),
        ],
        out_specs=[full] * NY,
    )


def back_body(place, grown, *refs):
    grads, out = refs[:NY], refs[NY]
    n = grads[0].shape[2]
    total = jnp.zeros(out.shape, F32)
    for k in range(NY):
        for h in range(ZH):
            first = (h * NY + lax.rem(place[0] - k + NY, NY)) * n
            total += dot(grads[k][h], grown[pl.ds(pl.multiple_of(first, n), n), :], NN)
    out[...] = total.astype(out.dtype)


def back_block(place, row_growth, grads):
    hidden, old = grads[0].shape[1], row_growth.shape[1]
    return call(
        back_body, place, (row_growth, *grads), struct((hidden, old), BF),
        2 * row_growth.size * hidden, limit=56,
    )


def inner_body(place, col, mine, other, *outs):
    block = pl.program_id(0)
    k = lax.rem(block - place[0] + NY, NY)
    put(dot(col[...], mine[...], NT), k, place[3], outs)
    put(dot(col[...], other[...], NT), k, 1 - place[3], outs)


def stream(rows, width):
    return pl.BlockSpec((rows, width), lambda s: (s, 0))


def keep_whole(shape):
    return pl.BlockSpec(shape, lambda s: (0,) * len(shape))


def inner_terms(place, col, source):
    hidden, width = col.shape
    rows = source[0].shape[0] // NY
    shape = (ZH, hidden, rows)
    outs = [struct(shape, F32)] + [struct(shape, BF)] * (NY - 1)
    return call(
        inner_body, place, (col, *source), outs, 4 * source[0].size * hidden,
        grid=(NY,),
        in_specs=[keep_whole(col.shape), stream(rows, width), stream(rows, width)],
        out_specs=[keep_whole(shape)] * NY,
    )


def col_body(place, mine, other, *refs):
    back, out, held = refs[:NY], refs[NY], refs[NY + 1]
    block = pl.program_id(0)

    @pl.when(block == 0)
    def _():
        for k in range(NY):
            held[k] = back[k][...]
        out[...] = jnp.zeros(out.shape, F32)

    k = lax.rem(place[0] - block + NY, NY)
    out[...] += dot(held[k, place[3]], mine[...], NN) + dot(held[k, 1 - place[3]], other[...], NN)


def col_grad(place, source, back):
    hidden, rows = back[0].shape[1:]
    width = source[0].shape[1]
    return call(
        col_body, place, (*source, *back), struct((hidden, width), F32),
        4 * source[0].size * hidden,
        scratch=[pltpu.VMEM((NY, *back[0].shape), BF)],
        limit=56,
        grid=(NY,),
        in_specs=[stream(rows, width)] * 2 + [keep_whole(back[0].shape)] * NY,
        out_specs=keep_whole((hidden, width)),
    )


def row_body(place, inner, *refs):
    grads, keep, give = refs[:NY], refs[NY], refs[NY + 1]
    rows = keep.shape[1]
    for k in range(NY):
        for h in range(ZH):
            block = dot(grads[k][h], inner[...], TN)
            at = (h * NY + lax.rem(place[0] - k + NY, NY)) * 2
            for q in range(2):
                one = block[2 * q * rows:(2 * q + 1) * rows]
                two = block[(2 * q + 1) * rows:(2 * q + 2) * rows]
                first = place[3] == 0
                keep[at + q] = jnp.where(first, one, two)
                give[at + q] = jnp.where(first, two, one).astype(BF)


def row_terms(place, inner, grads):
    old, n = inner.shape[1], grads[0].shape[2]
    shape = (NX * NZ, n * ZH * NY // MP, old)
    return call(
        row_body, place, (inner, *grads), [struct(shape, F32), struct(shape, BF)],
        2 * inner.size * n * ZH * NY,
    )


def out_body(place, mixed, *refs):
    inner, out = refs[:NY], refs[NY]
    total = jnp.zeros(out.shape, F32)
    for k in range(NY):
        for h in range(ZH):
            rows = mixed[:, h, k]
            total += dot(inner[k][h], rows.reshape(-1, out.shape[1]), NN)
    out[...] = total.astype(out.dtype)


def grown_output(place, mixed, inner):
    hidden, count = inner[0].shape[1], mixed.shape[-1]
    part = count // 4
    return call(
        out_body, place, (mixed, *inner), struct((hidden, count), BF),
        2 * mixed.size * hidden,
        limit=56,
        grid=(count // part,),
        in_specs=[pl.BlockSpec((*mixed.shape[:-1], part), lambda s: (0, 0, 0, 0, s))]
        + [keep_whole(inner[0].shape)] * NY,
        out_specs=pl.BlockSpec((hidden, part), lambda s: (0, s)),
    )


def together(*values):
    return lax.optimization_barrier(values)


def exchange_y(block_for):
    got = {k: lax.ppermute(block_for(k), "dp", shift_y(k)) for k in (2, 1, 3)}
    return [None, got[1], got[2], got[3]]


def sum_y(blocks):
    got = exchange_y(lambda k: blocks[k])
    return blocks[0] + got[1].astype(F32) + got[2].astype(F32) + got[3].astype(F32)


def sum_z(part):
    return part + lax.ppermute(part.astype(BF), "dp", SWAP_ZH).astype(F32)


def gather_y(block):
    return [block] + exchange_y(lambda k: block)[1:]


def panel_slots(saved, y):
    width = saved.shape[1]
    sub = saved.shape[0] // (MP * NY)
    rows = saved.reshape(NC, NX, NZ, NY, sub, width)
    mine = pick(rows, y, 3).transpose(1, 2, 0, 3, 4).reshape(MP, sub, width)
    return lax.all_to_all(mine, "mp", 0, 0)


def panel_rows(slots, slot_of, z_hi, y):
    sub, width = slots.shape[1:]
    mine = lax.dynamic_slice_in_dim(slot_of, z_hi * (MP // ZH), MP // ZH)
    panels = jnp.take(slots, mine, axis=0).reshape(NY, -1, sub, width)
    got = exchange_y(lambda k: pick(panels, (y + k) % NY))
    got[0] = pick(panels, y)
    chunk = jnp.stack([choose((y - j) % NY, got) for j in range(NY)])
    return chunk.transpose(0, 2, 1, 3).reshape(NY * sub, -1)


def gather(block, groups):
    blocks = jnp.broadcast_to(block[None], (len(groups[0]), *block.shape))
    return lax.all_to_all(blocks, "mp", 0, 0, axis_index_groups=groups).reshape(-1, *block.shape[1:])


def both_cores(half):
    return [half, lax.ppermute(half, "mp", SWAP_CORE)]


def own_strip(row_growth, z_hi, mp_index):
    old = row_growth.shape[1]
    strip = old // (NX * NZ)
    mine = pick(row_growth.T.reshape(NX * NZ, strip, -1), mp_index // NC)
    other = lax.ppermute(mine, "dp", SWAP_ZH)
    return jnp.where(z_hi == mp_index % NC, mine, other)


def shards(tokens, cotangent, saved_panels, owners, row_growth, col_growth):
    dp_index, mp_index = lax.axis_index("dp"), lax.axis_index("mp")
    z_hi, y = dp_index // NY, dp_index % NY
    x, core = mp_index // (NZ * NC), mp_index % NC
    place = jnp.stack([y, z_hi, x, core]).astype(jnp.int32)
    slot_of = owners[:, 1] * (MP // SECTIONS) + owners[:, 0]

    slots = panel_slots(saved_panels, y)
    part = sum_y(grad_terms(place, tokens, cotangent.T))
    strip = own_strip(row_growth, z_hi, mp_index)
    slots, part, strip = together(slots, part, strip)

    grads = sum_z(part)
    rows = panel_rows(slots, slot_of, z_hi, y)
    rows, grads, strip = together(rows, grads, strip)

    strips = jnp.concatenate(gather_y(strip))
    rows = gather(rows, Z_GROUPS)
    rows, grads, strips = together(rows, grads, strips)

    grad = pick(grads, z_hi).T
    grads = gather_y(grads.astype(BF))
    mixed = dot(strips, tokens, NT).astype(BF)
    half = gather(rows, X_GROUPS)
    half, grads, mixed = together(half, grads, mixed)

    mixed = lax.all_gather(mixed, "mp", axis=0, tiled=True)
    mixed = mixed.reshape(NX * NZ, NC, NY, -1, tokens.shape[0])
    source = both_cores(half)
    inners = inner_terms(place, col_growth, source)
    back = back_block(place, row_growth, grads)
    other = lax.ppermute(back, "dp", SWAP_ZH)
    pair = jnp.where(z_hi == 0, jnp.stack([back, other]), jnp.stack([other, back]))
    part, pair = together(sum_y(inners), pair)

    inners = sum_z(part)
    backs = gather_y(pair)
    inners, backs = together(inners, backs)

    inners = inners.astype(BF)
    keep, give = row_terms(place, pick(inners, z_hi), grads)
    keep = keep + lax.ppermute(give, "mp", SWAP_CORE).astype(F32)
    keep = lax.all_to_all(keep.astype(BF), "mp", 0, 0, axis_index_groups=PLANE_GROUPS)
    grad_row = keep.astype(F32).sum(axis=0)
    grad_col = col_grad(place, source, backs)
    inners = gather_y(inners)
    mixed, grad_col = together(mixed, grad_col)
    grown_out = grown_output(place, mixed, inners).T
    return (grown_out, grad, grad_row, grad_col)


def solution(mesh):
    in_specs = (P("dp", None), P("dp", "mp"), P(None, "mp"), P(), P(None, "dp"), P("mp", "dp"))
    out_specs = (P("dp", "mp"), P("dp", "mp"), P("mp", "dp"), P("mp", "dp"))
    return jax.shard_map(shards, mesh=mesh, in_specs=in_specs, out_specs=out_specs, check_vma=False)
```

```python
import jax
import jax.numpy as jnp
from jax import lax
from jax.experimental import pallas as pl
from jax.experimental.pallas import tpu as pltpu
from jax.sharding import PartitionSpec as P

SECTIONS = 4
ZH, NY = 2, 4
NX, NZ, NC = 4, 4, 2
MP = NX * NZ * NC
PLANE_GROUPS = [[(x * NZ + z) * NC + c for x in range(NX) for z in range(NZ)] for c in range(NC)]
X_GROUPS = [[(x * NZ + z) * NC + c for x in range(NX)] for z in range(NZ) for c in range(NC)]
Z_GROUPS = [[(x * NZ + z) * NC + c for z in range(NZ)] for x in range(NX) for c in range(NC)]
SWAP_ZH = [(i, (i + NY) % (ZH * NY)) for i in range(ZH * NY)]
SWAP_CORE = [(m, m ^ 1) for m in range(MP)]
BF, F32 = jnp.bfloat16, jnp.float32
NN, NT, TN = ((1,), (0,)), ((1,), (1,)), ((0,), (0,))


def shift_y(k):
    return [(h * NY + y, h * NY + (y + k) % NY) for h in range(ZH) for y in range(NY)]


def dot(a, b, dims):
    return lax.dot_general(a, b, (dims, ((), ())), preferred_element_type=F32)


def pick(blocks, index, axis=0):
    return lax.dynamic_index_in_dim(blocks, index, axis, keepdims=False)


def choose(index, cases):
    out = cases[-1]
    for at in range(len(cases) - 1):
        out = jnp.where(index == at, cases[at], out)
    return out


def call(body, place, arrays, outs, flops, scratch=(), limit=40, **specs):
    size = lambda s: s.size * s.dtype.itemsize
    whole = pl.BlockSpec(memory_space=pltpu.VMEM)
    return pl.pallas_call(
        body,
        out_shape=outs,
        grid=specs.get("grid", ()),
        in_specs=[pl.BlockSpec(memory_space=pltpu.SMEM)] + specs.get("in_specs", [whole] * len(arrays)),
        out_specs=specs.get("out_specs", jax.tree.map(lambda _: whole, outs)),
        scratch_shapes=list(scratch),
        compiler_params=pltpu.CompilerParams(vmem_limit_bytes=limit * 2**20),
        cost_estimate=pl.CostEstimate(
            flops=flops,
            bytes_accessed=sum(map(size, arrays)) + sum(map(size, jax.tree.leaves(outs))),
            transcendentals=0,
        ),
    )(place, *arrays)


def struct(shape, kind):
    return jax.ShapeDtypeStruct(shape, kind)


def put(value, k, at, outs):
    for case, out in enumerate(outs):
        @pl.when(k == case)
        def _():
            out[at] = value.astype(out.dtype)


def grad_body(place, tokens, cot, *outs):
    step = pl.program_id(0)
    both = dot(cot[...], tokens[...], NN)
    n = both.shape[1] // 2
    for half in range(2):
        block = 2 * step + half
        put(
            both[:, half * n:(half + 1) * n],
            lax.rem(lax.rem(block, NY) - place[0] + NY, NY),
            block // NY,
            outs,
        )


def grad_terms(place, tokens, cot):
    n = tokens.shape[1] // (ZH * NY)
    hidden = cot.shape[0]
    shape = (ZH, hidden, n)
    outs = [struct(shape, F32)] + [struct(shape, BF)] * (NY - 1)
    full = pl.BlockSpec(shape, lambda s: (0, 0, 0))
    return call(
        grad_body, place, (tokens, cot), outs, 2 * tokens.size * hidden,
        limit=56,
        grid=(ZH * NY // 2,),
        in_specs=[
            pl.BlockSpec((tokens.shape[0], 2 * n), lambda s: (0, s)),
            pl.BlockSpec(cot.shape, lambda s: (0, 0)),
        ],
        out_specs=[full] * NY,
    )


def back_body(place, grown, *refs):
    grads, out = refs[:NY], refs[NY]
    n = grads[0].shape[2]
    total = jnp.zeros(out.shape, F32)
    for k in range(NY):
        for h in range(ZH):
            first = (h * NY + lax.rem(place[0] - k + NY, NY)) * n
            total += dot(grads[k][h], grown[pl.ds(pl.multiple_of(first, n), n), :], NN)
    out[...] = total.astype(out.dtype)


def back_block(place, row_growth, grads):
    hidden, old = grads[0].shape[1], row_growth.shape[1]
    return call(
        back_body, place, (row_growth, *grads), struct((hidden, old), BF),
        2 * row_growth.size * hidden, limit=56,
    )


def inner_body(place, col, mine, other, *outs):
    block = pl.program_id(0)
    k = lax.rem(block - place[0] + NY, NY)
    put(dot(col[...], mine[...], NT), k, place[3], outs)
    put(dot(col[...], other[...], NT), k, 1 - place[3], outs)


def stream(rows, width):
    return pl.BlockSpec((rows, width), lambda s: (s, 0))


def keep_whole(shape):
    return pl.BlockSpec(shape, lambda s: (0,) * len(shape))


def inner_terms(place, col, source):
    hidden, width = col.shape
    rows = source[0].shape[0] // NY
    shape = (ZH, hidden, rows)
    outs = [struct(shape, F32)] + [struct(shape, BF)] * (NY - 1)
    return call(
        inner_body, place, (col, *source), outs, 4 * source[0].size * hidden,
        grid=(NY,),
        in_specs=[keep_whole(col.shape), stream(rows, width), stream(rows, width)],
        out_specs=[keep_whole(shape)] * NY,
    )


def col_body(place, mine, other, *refs):
    back, out, held = refs[:NY], refs[NY], refs[NY + 1]
    block = pl.program_id(0)

    @pl.when(block == 0)
    def _():
        for k in range(NY):
            held[k] = back[k][...]
        out[...] = jnp.zeros(out.shape, F32)

    k = lax.rem(place[0] - block + NY, NY)
    out[...] += dot(held[k, place[3]], mine[...], NN) + dot(held[k, 1 - place[3]], other[...], NN)


def col_grad(place, source, back):
    hidden, rows = back[0].shape[1:]
    width = source[0].shape[1]
    return call(
        col_body, place, (*source, *back), struct((hidden, width), F32),
        4 * source[0].size * hidden,
        scratch=[pltpu.VMEM((NY, *back[0].shape), BF)],
        limit=56,
        grid=(NY,),
        in_specs=[stream(rows, width)] * 2 + [keep_whole(back[0].shape)] * NY,
        out_specs=keep_whole((hidden, width)),
    )


def row_body(place, inner, *refs):
    grads, keep, give = refs[:NY], refs[NY], refs[NY + 1]
    rows = keep.shape[1]
    for k in range(NY):
        for h in range(ZH):
            block = dot(grads[k][h], inner[...], TN)
            at = (h * NY + lax.rem(place[0] - k + NY, NY)) * 2
            for q in range(2):
                one = block[2 * q * rows:(2 * q + 1) * rows]
                two = block[(2 * q + 1) * rows:(2 * q + 2) * rows]
                first = place[3] == 0
                keep[at + q] = jnp.where(first, one, two)
                give[at + q] = jnp.where(first, two, one).astype(BF)


def row_terms(place, inner, grads):
    old, n = inner.shape[1], grads[0].shape[2]
    shape = (NX * NZ, n * ZH * NY // MP, old)
    return call(
        row_body, place, (inner, *grads), [struct(shape, F32), struct(shape, BF)],
        2 * inner.size * n * ZH * NY,
    )


def out_body(place, mixed, *refs):
    inner, out = refs[:NY], refs[NY]
    total = jnp.zeros(out.shape, F32)
    for k in range(NY):
        for h in range(ZH):
            rows = mixed[:, h, k]
            total += dot(inner[k][h], rows.reshape(-1, out.shape[1]), NN)
    out[...] = total.astype(out.dtype)


def grown_output(place, mixed, inner):
    hidden, count = inner[0].shape[1], mixed.shape[-1]
    part = count // 4
    return call(
        out_body, place, (mixed, *inner), struct((hidden, count), BF),
        2 * mixed.size * hidden,
        limit=56,
        grid=(count // part,),
        in_specs=[pl.BlockSpec((*mixed.shape[:-1], part), lambda s: (0, 0, 0, 0, s))]
        + [keep_whole(inner[0].shape)] * NY,
        out_specs=pl.BlockSpec((hidden, part), lambda s: (0, s)),
    )


def together(*values):
    return lax.optimization_barrier(values)


def exchange_y(block_for):
    got = {k: lax.ppermute(block_for(k), "dp", shift_y(k)) for k in (2, 1, 3)}
    return [None, got[1], got[2], got[3]]


def sum_y(blocks):
    got = exchange_y(lambda k: blocks[k])
    return blocks[0] + got[1].astype(F32) + got[2].astype(F32) + got[3].astype(F32)


def sum_z(part):
    return part + lax.ppermute(part.astype(BF), "dp", SWAP_ZH).astype(F32)


def gather_y(block):
    return [block] + exchange_y(lambda k: block)[1:]


def panel_slots(saved, y):
    width = saved.shape[1]
    sub = saved.shape[0] // (MP * NY)
    rows = saved.reshape(NC, NX, NZ, NY, sub, width)
    mine = pick(rows, y, 3).transpose(1, 2, 0, 3, 4).reshape(MP, sub, width)
    return lax.all_to_all(mine, "mp", 0, 0)


def panel_rows(slots, slot_of, z_hi, y):
    sub, width = slots.shape[1:]
    mine = lax.dynamic_slice_in_dim(slot_of, z_hi * (MP // ZH), MP // ZH)
    panels = jnp.take(slots, mine, axis=0).reshape(NY, -1, sub, width)
    got = exchange_y(lambda k: pick(panels, (y + k) % NY))
    got[0] = pick(panels, y)
    chunk = jnp.stack([choose((y - j) % NY, got) for j in range(NY)])
    return chunk.transpose(0, 2, 1, 3).reshape(NY * sub, -1)


def gather(block, groups):
    blocks = jnp.broadcast_to(block[None], (len(groups[0]), *block.shape))
    return lax.all_to_all(blocks, "mp", 0, 0, axis_index_groups=groups).reshape(-1, *block.shape[1:])


def both_cores(half):
    return [half, lax.ppermute(half, "mp", SWAP_CORE)]


def own_strip(row_growth, z_hi, mp_index):
    old = row_growth.shape[1]
    strip = old // (NX * NZ)
    mine = pick(row_growth.T.reshape(NX * NZ, strip, -1), mp_index // NC)
    other = lax.ppermute(mine, "dp", SWAP_ZH)
    return jnp.where(z_hi == mp_index % NC, mine, other)


def shards(tokens, cotangent, saved_panels, owners, row_growth, col_growth):
    dp_index, mp_index = lax.axis_index("dp"), lax.axis_index("mp")
    z_hi, y = dp_index // NY, dp_index % NY
    x, core = mp_index // (NZ * NC), mp_index % NC
    place = jnp.stack([y, z_hi, x, core]).astype(jnp.int32)
    slot_of = owners[:, 1] * (MP // SECTIONS) + owners[:, 0]

    slots = panel_slots(saved_panels, y)
    part = sum_y(grad_terms(place, tokens, cotangent.T))
    strip = own_strip(row_growth, z_hi, mp_index)
    slots, part, strip = together(slots, part, strip)

    grads = sum_z(part)
    rows = panel_rows(slots, slot_of, z_hi, y)
    rows, grads, strip = together(rows, grads, strip)

    strips = jnp.concatenate(gather_y(strip))
    rows = gather(rows, Z_GROUPS)
    grad = pick(grads, z_hi).T
    rows, grads, strips = together(rows, grads.astype(BF), strips)

    grads = gather_y(grads)
    mixed = dot(strips, tokens, NT).astype(BF)
    half = gather(rows, X_GROUPS)
    half, grads, mixed = together(half, grads, mixed)

    mixed = lax.all_gather(mixed, "mp", axis=0, tiled=True)
    mixed = mixed.reshape(NX * NZ, NC, NY, -1, tokens.shape[0])
    source = both_cores(half)
    inners = inner_terms(place, col_growth, source)
    back = back_block(place, row_growth, grads)
    other = lax.ppermute(back, "dp", SWAP_ZH)
    pair = jnp.where(z_hi == 0, jnp.stack([back, other]), jnp.stack([other, back]))
    part, pair = together(sum_y(inners), pair)

    inners = sum_z(part)
    backs = gather_y(pair)
    inners, backs = together(inners, backs)

    inners = inners.astype(BF)
    keep, give = row_terms(place, pick(inners, z_hi), grads)
    keep = keep + lax.ppermute(give, "mp", SWAP_CORE).astype(F32)
    keep = lax.all_to_all(keep.astype(BF), "mp", 0, 0, axis_index_groups=PLANE_GROUPS)
    grad_row = keep.astype(F32).sum(axis=0)
    grad_col = col_grad(place, source, backs)
    inners = gather_y(inners)
    mixed, grad_col = together(mixed, grad_col)
    grown_out = grown_output(place, mixed, inners).T
    return (grown_out, grad, grad_row, grad_col)


def solution(mesh):
    in_specs = (P("dp", None), P("dp", "mp"), P(None, "mp"), P(), P(None, "dp"), P("mp", "dp"))
    out_specs = (P("dp", "mp"), P("dp", "mp"), P("mp", "dp"), P("mp", "dp"))
    return jax.shard_map(shards, mesh=mesh, in_specs=in_specs, out_specs=out_specs, check_vma=False)
```
